32 devices in a mesh: dp: 4 (over x, core), ctx: 4 (over z), mp: 2 (over y).
Axes of the slice: x: 2, y: 2, z: 4, core: 2. Of those that a mesh axis runs over, the one named last changes fastest.
Arguments:
- tokens: bfloat16 [8, 2048, 2048], P('dp', 'ctx'), may hold values from -40 to 40
- group_order: int32 [8, 8], P('dp'), may hold values from 0 to 7, each once within a row
- grad_out: bfloat16 [8, 2048, 2048], P('dp', 'ctx'), may hold values from -6 to 6
- norm_gain: bfloat16 [2048], P(('dp', 'ctx')), may hold values from 0.5 to 1.5
- norm_bias: bfloat16 [2048], P(('dp', 'ctx')), may hold values from -1.25 to 1.25
- w_qkv: bfloat16 [2048, 3, 2048], P(('dp', 'ctx'), None, 'mp'), may hold values from -0.125 to 0.125
- b_qkv: bfloat16 [3, 32, 64], P(None, 'mp', ('dp', 'ctx')), may hold values from -1.75 to 1.75
- w_out: bfloat16 [2048, 2048], P('mp', ('dp', 'ctx')), may hold values from -2 to 2
- b_out: bfloat16 [2048], P(('dp', 'ctx')), may hold values from -1.25 to 1.25
- w_fc1: bfloat16 [2048, 8192], P(('dp', 'ctx'), 'mp'), may hold values from -1 to 1
- b_fc1: bfloat16 [128, 64], P('mp', ('dp', 'ctx')), may hold values from -1.75 to 1.75
- w_fc2: bfloat16 [8192, 2048], P('mp', ('dp', 'ctx')), may hold values from -1 to 1
- b_fc2: bfloat16 [2048], P(('dp', 'ctx')), may hold values from -1.25 to 1.25
Outputs:
- block_out: bfloat16 [8, 2048, 2048], P('dp', 'ctx')
- grad_tokens: float32 [8, 2048, 2048], P('dp', 'ctx')
- grad_norm_gain: float32 [2048], P(('dp', 'ctx'))
- grad_norm_bias: float32 [2048], P(('dp', 'ctx'))
- grad_w_qkv: float32 [2048, 3, 2048], P(('dp', 'ctx'), None, 'mp')
- grad_b_qkv: float32 [3, 32, 64], P(None, 'mp', ('dp', 'ctx'))
- grad_w_out: float32 [2048, 2048], P('mp', ('dp', 'ctx'))
- grad_b_out: float32 [2048], P(('dp', 'ctx'))
- grad_w_fc1: float32 [2048, 8192], P(('dp', 'ctx'), 'mp')
- grad_b_fc1: float32 [128, 64], P('mp', ('dp', 'ctx'))
- grad_w_fc2: float32 [8192, 2048], P('mp', ('dp', 'ctx'))
- grad_b_fc2: float32 [2048], P(('dp', 'ctx'))
- root_means: float32 [3], replicated
The draws below stay inside these ranges and needn't reach their ends.
Inputs may be any that keep to these rules, and one draw needn't show every extreme that they name: `group_order`: each row lists every block of positions once.
All inputs are finite; a program needn't handle non-finite values.
Results may differ from the reference program's by a relative error of at most 0.019.
Values may be sent and summed in bfloat16 or wider, within the bound.
No kernel may reach another device: no remote copies, remote signals or barrier semaphores. Data moves between devices by JAX's collectives and lax.ppermute only.
A program may use at most 384 MiB of HBM per device.

```python
import jax
import jax.numpy as jnp
from jax import lax

D = 2048
HEADS = 32
HD = 64
ROT = 32
FF = 8192
SEQ_LEN = 2048
NSEQ = 8
GROUPS = 8


def draw_tokens(key, part):
    rank = jnp.arange(NSEQ, dtype=jnp.float32) / max(NSEQ - 1, 1)
    base = jnp.clip(jax.random.normal(jax.random.fold_in(key, 13), (NSEQ, SEQ_LEN, D), jnp.float32), -4.0, 4.0)
    seq_scale = jnp.sqrt(1.0 + 2.0 * rank)
    column_scale = jnp.exp(jax.random.uniform(jax.random.fold_in(key, 14), (D,), jnp.float32, -0.7, 0.7))
    return (base * seq_scale[:, None, None] * column_scale[None, None, :]).astype(jnp.bfloat16)


def draw_w_fc1(key, part):
    key = jax.random.fold_in(key, 31)
    entry_key = jax.random.fold_in(key, 1)
    column_key = jax.random.fold_in(key, 2)
    base = jnp.clip(jax.random.normal(entry_key, (D, FF), jnp.float32), -4.0, 4.0)
    column_part = 0.5 * jnp.clip(jax.random.normal(column_key, (FF,), jnp.float32), -3.0, 3.0)
    return ((base + column_part[None, :]) * D ** (-0.5)).astype(jnp.bfloat16)


def draw_w_fc2(key, part):
    key = jax.random.fold_in(key, 21)
    column_place = jnp.arange(D, dtype=jnp.float32) / max(D - 1, 1)
    column_scale = jnp.exp(column_place * jnp.log(3.0)) / 1.9
    base = jnp.clip(jax.random.normal(key, (FF, D), jnp.float32), -4.0, 4.0)
    return (base * column_scale[None, :] * FF ** (-0.5)).astype(jnp.bfloat16)


def block_levels(stream_key, extent, cuts, smallest, high):
    loudness = 1.0
    for dim, shards_of in cuts:
        heights = jax.random.uniform(jax.random.fold_in(jax.random.fold_in(stream_key, 6), dim), (shards_of,), jnp.float32, smallest / len(cuts), high / len(cuts))
        loudness = loudness * jnp.repeat(jnp.exp(heights), extent[dim] // shards_of).reshape((-1,) + (1,) * (len(extent) - 1 - dim))
    return loudness


def gaussian(stream_key, dims, deviation, most, split=(), held_as=jnp.bfloat16):
    level = block_levels(stream_key, dims, split, -0.22, 0.18) if split else 1.0
    drawn = jax.random.normal(stream_key, dims, jnp.float32) * deviation * level
    return jnp.minimum(jnp.maximum(drawn, -most), most).astype(held_as)


def setup_inputs(seed: int = 0) -> dict:
    arg_keys = jax.random.split(jax.random.key(seed), 14)
    tokens = draw_tokens(jax.random.fold_in(arg_keys[13], 71), 0)
    group_order = jax.vmap(lambda own: jax.random.permutation(own, GROUPS))(jax.random.split(arg_keys[1], NSEQ)).reshape((NSEQ, GROUPS)).astype(jnp.int32)
    grad_out = gaussian(arg_keys[2], (NSEQ, SEQ_LEN, D), 1.0, 6.0, ((0, 4), (1, 4)))
    norm_gain = jnp.clip(1.0 + 0.1 * jax.random.normal(arg_keys[3], (D,), jnp.float32), 0.5, 1.5).astype(jnp.bfloat16)
    norm_bias = gaussian(arg_keys[4], (D,), 0.2, 1.25, ((0, 16),))
    w_qkv = gaussian(arg_keys[5], (D, 3, D), D ** -0.5, 0.125, ((0, 16), (2, 2)))
    b_qkv = gaussian(arg_keys[6], (3, HEADS, HD), 0.3, 1.75, ((1, 2), (2, 16)))
    w_out = gaussian(arg_keys[7], (D, D), (D * 8 // SEQ_LEN) ** -0.5, 2.0, ((0, 2), (1, 16)))
    b_out = gaussian(arg_keys[8], (D,), 0.2, 1.25, ((0, 16),))
    w_fc1 = draw_w_fc1(jax.random.fold_in(arg_keys[13], 71), 0)
    b_fc1 = gaussian(arg_keys[10], (FF // HD, HD), 0.3, 1.75, ((0, 2), (1, 16)))
    w_fc2 = draw_w_fc2(jax.random.fold_in(arg_keys[13], 71), 0)
    b_fc2 = gaussian(arg_keys[12], (D,), 0.2, 1.25, ((0, 16),))
    return {"tokens": tokens, "group_order": group_order, "grad_out": grad_out, "norm_gain": norm_gain, "norm_bias": norm_bias, "w_qkv": w_qkv, "b_qkv": b_qkv, "w_out": w_out, "b_out": b_out, "w_fc1": w_fc1, "b_fc1": b_fc1, "w_fc2": w_fc2, "b_fc2": b_fc2}


norm_eps = 1e-05
rotary_base = 10000.0
masked_fill = -1e+30
highest = lax.Precision.HIGHEST

@jax.custom_vjp
def low(v):
    return lax.optimization_barrier(v.astype(jnp.bfloat16)).astype(jnp.float32)

@jax.custom_vjp
def low_back(v):
    return v

def low_keep(v):
    return (low(v), None)

def low_pass(kept, grad):
    return (grad,)

def back_keep(v):
    return (v, None)

def back_low(kept, grad):
    return (low(grad),)
low.defvjp(low_keep, low_pass)
low_back.defvjp(back_keep, back_low)

def slot_positions(order_row):
    block_len = SEQ_LEN // GROUPS
    slot_ids = jnp.arange(SEQ_LEN, dtype=jnp.int32)
    return order_row[slot_ids // block_len] * block_len + slot_ids % block_len

def rotary_tables(positions):
    half_rot = ROT // 2
    inverse = jnp.power(rotary_base, -jnp.arange(half_rot, dtype=jnp.float32) * (2.0 / ROT))
    angles = positions.astype(jnp.float32)[..., None] * inverse
    return (jnp.cos(angles)[..., None, :], jnp.sin(angles)[..., None, :])

def rotate(values, cosine_table, sine_table):
    half_rot = ROT // 2
    first = values[..., :half_rot]
    second = values[..., half_rot:ROT]
    return jnp.concatenate([first * cosine_table - second * sine_table, second * cosine_table + first * sine_table, values[..., ROT:]], axis=-1)

def sequence_layer(params, row_in, positions):
    norm_gain, norm_bias, w_qkv, b_qkv, w_out, b_out, w_fc1, b_fc1, w_fc2, b_fc2 = params
    row_mean = lax.optimization_barrier(jnp.mean(row_in, axis=-1, keepdims=True))
    centered = row_in - row_mean
    variance = lax.optimization_barrier(jnp.mean(centered * centered, axis=-1, keepdims=True))
    normed = centered * lax.rsqrt(variance + norm_eps)
    ln_out = low(normed * norm_gain + norm_bias)
    qkv_proj = low_back(jnp.einsum('td,dcf->tcf', ln_out, w_qkv, precision=highest) + b_qkv.reshape(3, D))
    cosine_table, sine_table = rotary_tables(positions)
    queries = low(rotate(qkv_proj[:, 0].reshape(SEQ_LEN, HEADS, HD), cosine_table, sine_table))
    keys_all = low(rotate(qkv_proj[:, 1].reshape(SEQ_LEN, HEADS, HD), cosine_table, sine_table))
    values_all = low(qkv_proj[:, 2].reshape(SEQ_LEN, HEADS, HD))
    scores = low_back(jnp.einsum('qhd,khd->hqk', queries, keys_all, precision=highest) * HD ** (-0.5))
    allowed = positions[None, :] <= positions[:, None]
    masked = jnp.where(allowed[None], scores, masked_fill)
    probs = low(jax.nn.softmax(masked, axis=-1))
    attention = jnp.einsum('hqk,khd->qhd', probs, values_all, precision=highest)
    mixed = low(low_back(attention)).reshape(SEQ_LEN, D)
    attn_out = jnp.dot(mixed, w_out, precision=highest) + b_out
    pre_act = low_back(jnp.dot(ln_out, w_fc1, precision=highest) + b_fc1.reshape(FF))
    activation = low(jax.nn.gelu(pre_act, approximate=True))
    mlp_out = jnp.dot(activation, w_fc2, precision=highest) + b_fc2
    block = row_in + attn_out + mlp_out
    return (block, jnp.stack([jnp.sum(attn_out * attn_out), jnp.sum(mlp_out * mlp_out)]))

def whole_layer(tokens_in, params, positions):

    def one_sequence(packed):
        return sequence_layer(params, packed[0], packed[1])
    blocks, square_sums = lax.map(jax.checkpoint(one_sequence), (tokens_in, positions))
    return (blocks, lax.optimization_barrier(jnp.sum(square_sums, axis=0)))

def reference(tokens, group_order, grad_out, norm_gain, norm_bias, w_qkv, b_qkv, w_out, b_out, w_fc1, b_fc1, w_fc2, b_fc2):
    params = (norm_gain.astype(jnp.float32), norm_bias.astype(jnp.float32), w_qkv.astype(jnp.float32), b_qkv.astype(jnp.float32), w_out.astype(jnp.float32), b_out.astype(jnp.float32), w_fc1.astype(jnp.float32), b_fc1.astype(jnp.float32), w_fc2.astype(jnp.float32), b_fc2.astype(jnp.float32))
    tokens_in = tokens.astype(jnp.float32)
    positions = jax.vmap(slot_positions)(group_order)

    def layer_of(inputs_now, params_now):
        return whole_layer(inputs_now, params_now, positions)
    blocks, pull, square_sums = jax.vjp(layer_of, tokens_in, params, has_aux=True)
    grad_in, grad_params = pull(grad_out.astype(jnp.float32))
    totals = jnp.stack([jnp.sum(tokens_in * tokens_in), square_sums[0], square_sums[1]])
    root_means = jnp.sqrt(totals / (NSEQ * SEQ_LEN * D))
    return (blocks.astype(jnp.bfloat16), grad_in, grad_params[0], grad_params[1], grad_params[2], grad_params[3], grad_params[4], grad_params[5], grad_params[6], grad_params[7], grad_params[8], grad_params[9], root_means)
```

```python
from functools import partial

import jax
import jax.numpy as jnp
from jax import lax
from jax.experimental import pallas as pl
from jax.experimental.pallas import tpu as pltpu
from jax.sharding import PartitionSpec as P

HD = 64
ROT = 32
SEQ_LEN = 2048
PAIR = 2 * HD
TILE = 256

norm_eps = 1e-05
rotary_base = 10000.0
masked_fill = -1e30
low = jnp.bfloat16
wide = jnp.float32


def rotary_rows(seq):
    half = ROT // 2
    lane = jnp.arange(PAIR, dtype=jnp.int32)[None, :] % HD
    inverse = jnp.power(rotary_base, -(lane % half).astype(wide) * (2.0 / ROT))
    angles = jnp.arange(seq, dtype=wide)[:, None] * inverse
    cosine, sine = jnp.cos(angles), jnp.sin(angles)
    return (
        jnp.where(lane < ROT, cosine, 1.0),
        jnp.where(lane < half, -sine, 0.0),
        jnp.where((lane >= half) & (lane < ROT), sine, 0.0),
    )


def attention_kernel(
    order_ref, qkv_ref, do_ref, cos_ref, up_ref, down_ref, mixed_ref, grad_ref,
    sorted_qkv, sorted_do, q_nat, k_nat, v_nat, do_nat, q_t, k_t, v_t, do_t,
    s_ref, dk_acc, dv_acc, out_s, grad_s, *, pieces, piece,
):
    blocks = pieces * piece // TILE
    scale = HD**-0.5
    dot = partial(jnp.dot, preferred_element_type=wide)

    def rows_of(b):
        return pl.ds(pl.multiple_of(b * TILE, TILE), TILE)

    def fold(t, how):
        return how(t.reshape(TILE // 8, 8, TILE), axis=0)

    def gather(r, _):
        src = pl.multiple_of(order_ref[r] * piece, piece)
        dst = pl.multiple_of(r * piece, piece)
        sorted_qkv[pl.ds(dst, piece), :] = qkv_ref[pl.ds(src, piece), :]
        sorted_do[pl.ds(dst, piece), :] = do_ref[pl.ds(src, piece), :]
        return 0

    lax.fori_loop(0, pieces, gather, 0)
    first = lax.broadcasted_iota(jnp.int32, (TILE, PAIR), 1) < HD

    def turn(t, rows, sign):
        up = pltpu.roll(t, PAIR - ROT // 2, 1) * up_ref[rows, :]
        down = pltpu.roll(t, ROT // 2, 1) * down_ref[rows, :]
        return t * cos_ref[rows, :] + sign * (up + down)

    def prepare(b, _):
        rows = rows_of(b)
        q = turn(sorted_qkv[rows, 0:PAIR], rows, 1.0).astype(low).astype(wide) * scale
        k = turn(sorted_qkv[rows, PAIR : 2 * PAIR], rows, 1.0)
        v = sorted_qkv[rows, 2 * PAIR : 3 * PAIR]
        g = sorted_do[rows, :].astype(wide)
        for val, nat, tr in ((q, q_nat, q_t), (k, k_nat, k_t), (v, v_nat, v_t), (g, do_nat, do_t)):
            nat[0, b] = jnp.where(first, val, 0.0).astype(low)
            nat[1, b] = jnp.where(first, 0.0, val).astype(low)
            tr[b] = val.T.astype(low)
        dk_acc[b] = jnp.zeros((TILE, PAIR), wide)
        dv_acc[b] = jnp.zeros((TILE, PAIR), wide)
        return 0

    lax.fori_loop(0, blocks, prepare, 0)
    key_row = lax.broadcasted_iota(jnp.int32, (TILE, TILE), 0)
    query_col = lax.broadcasted_iota(jnp.int32, (TILE, TILE), 1)
    allowed = key_row <= query_col

    def one_block(i, _):
        q_i = q_t[i]
        do_i = do_t[i]

        def score(j, tops):
            new = []
            for h in range(2):
                s = dot(k_nat[h, j], q_i)
                s_ref[h, j] = s
                new.append(jnp.maximum(tops[h], fold(s, jnp.max)))
            return tuple(new)

        partial_tops = lax.fori_loop(
            0, i, score, (jnp.full((8, TILE), masked_fill, wide),) * 2
        )
        tops = []
        for h in range(2):
            s = jnp.where(allowed, dot(k_nat[h, i], q_i), masked_fill)
            s_ref[h, i] = s
            tops.append(
                jnp.max(jnp.maximum(partial_tops[h], fold(s, jnp.max)), axis=0, keepdims=True)
            )

        def weigh(j, carry):
            sums, accs = carry
            new_sums, new_accs = [], []
            for h in range(2):
                p = jnp.exp(s_ref[h, j] - tops[h])
                s_ref[h, j] = p
                new_sums.append(sums[h] + fold(p, jnp.sum))
                new_accs.append(accs[h] + dot(v_t[j, h * HD : (h + 1) * HD, :], p.astype(low)))
            return tuple(new_sums), tuple(new_accs)

        sums, accs = lax.fori_loop(
            0,
            i + 1,
            weigh,
            ((jnp.zeros((8, TILE), wide),) * 2, (jnp.zeros((HD, TILE), wide),) * 2),
        )
        invs, deltas, outs = [], [], []
        for h in range(2):
            inv = 1.0 / jnp.sum(sums[h], axis=0, keepdims=True)
            o = accs[h] * inv
            outs.append(o)
            invs.append(inv)
            g = do_i[h * HD : (h + 1) * HD, :].astype(wide)
            deltas.append(jnp.sum(o * g, axis=0, keepdims=True))
        out_s[i] = jnp.concatenate(outs, axis=0).T.astype(low)

        def pull(j, dq):
            new = []
            dv = dk = None
            for h in range(2):
                dp = dot(v_nat[h, j], do_i)
                p = s_ref[h, j] * invs[h]
                ds = (p * (dp - deltas[h])).astype(low)
                dv_h = dot(p.astype(low), do_nat[h, i])
                dk_h = dot(ds, q_nat[h, i])
                dv = dv_h if dv is None else dv + dv_h
                dk = dk_h if dk is None else dk + dk_h
                new.append(dq[h] + dot(k_t[j, h * HD : (h + 1) * HD, :], ds))
            dv_acc[j] += dv
            dk_acc[j] += dk
            return tuple(new)

        dq = lax.fori_loop(0, i + 1, pull, (jnp.zeros((HD, TILE), wide),) * 2)
        rows = rows_of(i)
        dq_rows = jnp.concatenate(dq, axis=0).T * scale
        grad_s[rows, 0:PAIR] = turn(dq_rows, rows, -1.0).astype(low)
        return 0

    lax.fori_loop(0, blocks, one_block, 0)

    def finish(b, _):
        rows = rows_of(b)
        grad_s[rows, PAIR : 2 * PAIR] = turn(dk_acc[b], rows, -1.0).astype(low)
        grad_s[rows, 2 * PAIR : 3 * PAIR] = dv_acc[b].astype(low)
        sorted_do[rows, :] = out_s[b]
        return 0

    lax.fori_loop(0, blocks, finish, 0)

    def scatter(r, _):
        src = pl.multiple_of(order_ref[r] * piece, piece)
        dst = pl.multiple_of(r * piece, piece)
        mixed_ref[pl.ds(src, piece), :] = sorted_do[pl.ds(dst, piece), :]
        grad_ref[pl.ds(src, piece), :] = grad_s[pl.ds(dst, piece), :]
        return 0

    lax.fori_loop(0, pieces, scatter, 0)


def attention(order, qkv, grad_mixed):
    seq, width = grad_mixed.shape
    pairs = width // PAIR
    pieces = order.shape[0]
    blocks = seq // TILE
    vmem = pltpu.VMEM
    table = pl.BlockSpec((seq, PAIR), lambda p, o: (0, 0))
    one = pl.BlockSpec((seq, PAIR), lambda p, o: (0, p))
    three = pl.BlockSpec((seq, 3 * PAIR), lambda p, o: (0, p))
    return pl.pallas_call(
        partial(attention_kernel, pieces=pieces, piece=seq // pieces),
        grid_spec=pltpu.PrefetchScalarGridSpec(
            num_scalar_prefetch=1,
            grid=(pairs,),
            in_specs=[three, one, table, table, table],
            out_specs=[one, three],
            scratch_shapes=[
                vmem((seq, 3 * PAIR), wide),
                vmem((seq, PAIR), low),
                *[vmem((2, blocks, TILE, PAIR), low)] * 4,
                *[vmem((blocks, PAIR, TILE), low)] * 4,
                vmem((2, blocks, TILE, TILE), wide),
                vmem((blocks, TILE, PAIR), wide),
                vmem((blocks, TILE, PAIR), wide),
                vmem((blocks, TILE, PAIR), low),
                vmem((seq, 3 * PAIR), low),
            ],
        ),
        out_shape=[
            jax.ShapeDtypeStruct((seq, width), low),
            jax.ShapeDtypeStruct((seq, 3 * width), low),
        ],
        compiler_params=pltpu.CompilerParams(
            vmem_limit_bytes=48 * 1024 * 1024, dimension_semantics=("arbitrary",)
        ),
        cost_estimate=pl.CostEstimate(
            flops=pairs * 24 * seq * seq * PAIR, bytes_accessed=30_000_000, transcendentals=0
        ),
        name="attention",
    )(order, qkv, grad_mixed, *rotary_rows(seq))


def mm(a, b):
    return jnp.dot(a, b, preferred_element_type=wide)


def mm_nt(a, b):
    return lax.dot_general(a, b, (((1,), (1,)), ((), ())), preferred_element_type=wide)


def mm_tn(a, b):
    return lax.dot_general(a, b, (((0,), (0,)), ((), ())), preferred_element_type=wide)


def on_device(
    tokens,
    group_order,
    grad_out,
    norm_gain,
    norm_bias,
    w_qkv,
    b_qkv,
    w_out,
    b_out,
    w_fc1,
    b_fc1,
    w_fc2,
    b_fc2,
):
    n_dp, n_ctx, n_mp = lax.axis_size("dp"), lax.axis_size("ctx"), lax.axis_size("mp")
    n_seq, n_slot, model = tokens.shape
    groups = group_order.shape[1]
    assert n_dp == 4 and 2 * n_seq == n_ctx == 4
    dp, z, y = lax.axis_index("dp"), lax.axis_index("ctx"), lax.axis_index("mp")
    x, c = dp // 2, dp % 2
    half = model // 2
    part = n_slot // (2 * n_mp)
    rows_own = n_ctx * part
    block_len = SEQ_LEN // groups

    def to_core(v):
        return lax.ppermute(v, "dp", [(i, i ^ 1) for i in range(n_dp)])

    def to_x(v):
        return lax.ppermute(v, "dp", [(i, i ^ 2) for i in range(n_dp)])

    def by_core(mine, other, axis):
        return jnp.where(
            c == 0,
            jnp.concatenate([mine, other], axis),
            jnp.concatenate([other, mine], axis),
        )

    def roll_x(v):
        return jnp.where(x == 0, v, jnp.concatenate([v[..., half:], v[..., :half]], axis=-1))

    d_own = w_qkv.shape[0]
    pairs = w_qkv.shape[2] // PAIR // 2
    qkv_cols = pairs * 3 * PAIR
    out_cols = pairs * PAIR
    hid = w_fc1.shape[1] // 2
    qkv_split = w_qkv.reshape(d_own, 3, 2, pairs, PAIR).transpose(2, 0, 3, 1, 4)
    qkv_split = qkv_split.reshape(2, d_own, qkv_cols)
    out_split = w_out.T.reshape(d_own, 2, out_cols).transpose(1, 0, 2)
    heads_split = jnp.concatenate([qkv_split, out_split], axis=-1)
    fc1_split = w_fc1.reshape(d_own, 2, hid).transpose(1, 0, 2)
    fc2_split = w_fc2.T.reshape(d_own, 2, hid).transpose(1, 0, 2)

    def gather_weight(split):
        mine = lax.dynamic_index_in_dim(split, c, 0, keepdims=True)
        other = to_core(lax.dynamic_index_in_dim(split, 1 - c, 0, keepdims=True))
        both = by_core(mine, other, 0)
        near = lax.all_gather(both, "ctx", axis=1, tiled=True).reshape(half, split.shape[-1])
        return near, to_x(near)

    heads_near, heads_far = gather_weight(heads_split)
    fc1_near, fc1_far = gather_weight(fc1_split)
    fc2_near, fc2_far = gather_weight(fc2_split)

    small = jnp.concatenate(
        [
            norm_gain,
            norm_bias,
            b_out,
            b_fc2,
            b_qkv.reshape(-1),
            b_fc1.reshape(-1),
        ]
    )
    small_all = lax.all_gather(small, ("dp", "ctx"), axis=0, tiled=False)
    n_own = n_dp * n_ctx
    at = 0

    def take(count):
        nonlocal at
        got = small_all[:, at : at + count]
        at += count
        return got

    gain = roll_x(take(d_own).reshape(model).astype(wide))
    shift = roll_x(take(d_own).reshape(model).astype(wide))
    out_bias = roll_x(take(d_own).reshape(model).astype(wide))
    fc2_bias = roll_x(take(d_own).reshape(model).astype(wide))
    heads_here = b_qkv.shape[1]
    dims_here = b_qkv.shape[2]
    qkv_bias = take(b_qkv.size).reshape(n_own, 3, heads_here, dims_here)
    qkv_bias = qkv_bias.transpose(1, 2, 0, 3).reshape(3, 2, pairs, PAIR)
    qkv_bias = lax.dynamic_index_in_dim(qkv_bias, c, 1, keepdims=False)
    qkv_bias = qkv_bias.transpose(1, 0, 2).reshape(qkv_cols).astype(wide)
    fc1_bias = take(b_fc1.size).reshape(n_own, b_fc1.shape[0], b_fc1.shape[1])
    fc1_bias = fc1_bias.transpose(1, 0, 2).reshape(2, hid)
    fc1_bias = lax.dynamic_index_in_dim(fc1_bias, c, 0, keepdims=False).astype(wide)

    def away(k):
        return [
            (
                (2 * xx + cc) * n_ctx + zz,
                (2 * xx + (zz ^ k) // 2) * n_ctx + 2 * cc + (zz ^ k) % 2,
            )
            for xx in range(2)
            for cc in range(2)
            for zz in range(n_ctx)
        ]

    def send_away(v):
        cut = v.reshape(n_seq, 2, n_mp, part, model)
        got = []
        for k in range(n_ctx):
            there = z ^ k
            piece = lax.dynamic_slice(
                cut, (there % 2, there // 2, y, 0, 0), (1, 1, 1, part, model)
            ).reshape(part, model)
            got.append(lax.ppermute(roll_x(piece), ("dp", "ctx"), away(k)))
        return jnp.concatenate(got, axis=0)

    def send_home(v):
        cut = v.reshape(n_ctx, part, model)
        homes = []
        for k in range(n_ctx):
            back = [(b, a) for a, b in away(k)]
            piece = lax.ppermute(roll_x(cut[k]), ("dp", "ctx"), back)
            if n_mp == 2:
                other = lax.ppermute(piece, "mp", [(0, 1), (1, 0)])
                piece = jnp.where(
                    y == 0,
                    jnp.concatenate([piece, other], axis=0),
                    jnp.concatenate([other, piece], axis=0),
                )
            else:
                piece = lax.all_gather(piece, "mp", axis=0, tiled=True)
            homes.append(piece)
        stacked = jnp.stack(homes, axis=0)
        placed = [
            lax.dynamic_index_in_dim(stacked, (2 * cc + i) ^ z, 0, keepdims=False)
            for i in range(n_seq)
            for cc in range(2)
        ]
        return jnp.stack(placed, axis=0).reshape(n_seq, n_slot, model)

    def gather_rows(own):
        if n_mp == 2:
            own = jnp.concatenate([own, lax.ppermute(own, "mp", [(0, 1), (1, 0)])], axis=0)
        else:
            own = lax.all_gather(own, "mp", axis=0, tiled=True)
        return jnp.concatenate([own, to_core(own)], axis=0)

    def sum_rows(left, right):
        split = left.shape[0] // 2
        far = to_core(mm_nt(left[split:], right).astype(low))
        near = mm_nt(left[:split], right) + far.astype(wide)
        if n_mp == 2:
            other = lax.ppermute(near[rows_own:].astype(low), "mp", [(0, 1), (1, 0)])
            return near[:rows_own] + other.astype(wide)
        return lax.psum_scatter(near.astype(low), "mp", scatter_dimension=0, tiled=True).astype(wide)

    rows_in = send_away(tokens)
    rows_grad = send_away(grad_out)

    tokens_in = rows_in.astype(wide)
    row_mean = jnp.mean(tokens_in, axis=-1, keepdims=True)
    centered = tokens_in - row_mean
    variance = jnp.mean(centered * centered, axis=-1, keepdims=True)
    inv_std = lax.rsqrt(variance + norm_eps)
    normed = centered * inv_std
    ln_out = gather_rows((normed * gain + shift).astype(low))
    grad_rows = gather_rows(rows_grad)

    other_order = to_core(group_order)
    order_row = jnp.where(z // 2 == c, group_order, other_order)
    order_row = lax.dynamic_index_in_dim(order_row, z % 2, 0, keepdims=False)
    ids = jnp.arange(2 * n_mp * n_ctx, dtype=jnp.int32)
    at_core = (ids // (n_mp * n_ctx)) ^ c
    at_mp = (ids // n_ctx) % n_mp
    at_mp = at_mp ^ y if n_mp == 2 else at_mp
    at_ctx = (2 * at_core + z % 2) ^ (ids % n_ctx)
    slot = at_ctx * n_slot + at_core * (n_slot // 2) + at_mp * part
    position = order_row[slot // block_len] * block_len + slot % block_len
    order = jnp.sum(jnp.where((position // part)[None, :] == ids[:, None], ids[None, :], 0), axis=1)

    heads_w = jnp.concatenate([heads_near, heads_far], axis=0)
    qkv_w, out_w = heads_w[:, :qkv_cols], heads_w[:, qkv_cols:]
    qkv = mm(ln_out, qkv_w) + qkv_bias
    grad_mixed = mm(grad_rows, out_w).astype(low)
    mixed, grad_qkv = attention(order, qkv, grad_mixed)
    attn_out = sum_rows(mixed, out_w) + out_bias

    def scatter_weight(far, near):
        cols = near.shape[1]
        total = (near + to_x(far.astype(low)).astype(wide)).astype(low)
        mine = lax.psum_scatter(
            total.reshape(2, half // 2, cols), "ctx", scatter_dimension=1, tiled=True
        )
        other = to_core(lax.dynamic_index_in_dim(mine, 1 - c, 0, keepdims=True))
        mine = lax.dynamic_index_in_dim(mine, c, 0, keepdims=True)
        return by_core(mine, other, 0).astype(wide)

    def weight_grad(left, right):
        return mm_tn(left[:, half:], right), mm_tn(left[:, :half], right)

    grad_qkv_w = scatter_weight(*weight_grad(ln_out, grad_qkv))
    grad_out_w = scatter_weight(*weight_grad(grad_rows, mixed))

    fc1_w = jnp.concatenate([fc1_near, fc1_far], axis=0)
    fc2_w = jnp.concatenate([fc2_near, fc2_far], axis=0)
    pre_act = mm(ln_out, fc1_w) + fc1_bias
    gelu = partial(jax.nn.gelu, approximate=True)
    act = gelu(pre_act).astype(low)
    grad_fc2_w = scatter_weight(*weight_grad(grad_rows, act))
    mlp_out = sum_rows(act, fc2_w) + fc2_bias
    grad_act = mm(grad_rows, fc2_w)
    grad_pre = jax.vjp(gelu, pre_act)[1](grad_act)[0].astype(low)
    grad_fc1_w = scatter_weight(*weight_grad(ln_out, grad_pre))

    block_out = send_home((tokens_in + attn_out + mlp_out).astype(low))
    grad_ln = sum_rows(
        jnp.concatenate([grad_pre, grad_qkv], axis=1), jnp.concatenate([fc1_w, qkv_w], axis=1)
    )
    grad_scaled = grad_ln * gain
    grad_norm = inv_std * (
        grad_scaled
        - jnp.mean(grad_scaled, axis=-1, keepdims=True)
        - normed * jnp.mean(grad_scaled * normed, axis=-1, keepdims=True)
    )
    grad_tokens = grad_out.astype(wide) + send_home(grad_norm.astype(low)).astype(wide)

    shared = jnp.concatenate(
        [
            roll_x(jnp.sum(grad_ln * normed, axis=0)),
            roll_x(jnp.sum(grad_ln, axis=0)),
            roll_x(jnp.sum(rows_grad.astype(wide), axis=0)),
            jnp.stack(
                [
                    jnp.sum(tokens_in * tokens_in),
                    jnp.sum(attn_out * attn_out),
                    jnp.sum(mlp_out * mlp_out),
                ]
            ),
        ]
    )
    shared = lax.psum(shared, ("dp", "ctx", "mp"))
    own = jnp.concatenate(
        [jnp.sum(grad_qkv.astype(wide), axis=0), jnp.sum(grad_pre.astype(wide), axis=0)]
    )
    own = own + to_x(own)
    own = lax.psum(own, "ctx")
    own = by_core(own[None], to_core(own)[None], 0)
    place = dp * n_ctx + z

    def own_slice(v):
        return lax.dynamic_slice_in_dim(v, place * d_own, d_own, 0)

    grad_gain = own_slice(shared[:model])
    grad_shift = own_slice(shared[model : 2 * model])
    grad_bias_out = own_slice(shared[2 * model : 3 * model])
    cells = n_dp * n_seq * SEQ_LEN * model
    root_means = jnp.sqrt(shared[3 * model :] / cells)
    grad_b_qkv = own[:, :qkv_cols].reshape(2, pairs, 3, PAIR).transpose(2, 0, 1, 3)
    grad_b_qkv = grad_b_qkv.reshape(3, heads_here, HD)
    grad_b_qkv = lax.dynamic_slice_in_dim(grad_b_qkv, place * dims_here, dims_here, 2)
    grad_b_fc1 = own[:, qkv_cols:].reshape(b_fc1.shape[0], HD)
    grad_b_fc1 = lax.dynamic_slice_in_dim(grad_b_fc1, place * dims_here, dims_here, 1)

    def join(v):
        return v.transpose(1, 0, 2).reshape(d_own, -1)

    grad_qkv_w = grad_qkv_w.reshape(2, d_own, pairs, 3, PAIR).transpose(1, 3, 0, 2, 4)
    return (
        block_out,
        grad_tokens,
        grad_gain,
        grad_shift,
        grad_qkv_w.reshape(d_own, 3, -1),
        grad_b_qkv,
        join(grad_out_w).T,
        grad_bias_out,
        join(grad_fc1_w),
        grad_b_fc1,
        join(grad_fc2_w).T,
        grad_bias_out,
        root_means,
    )


def solution(mesh):
    owners = ("dp", "ctx")
    return jax.shard_map(
        on_device,
        mesh=mesh,
        in_specs=(
            P("dp", "ctx", None),
            P("dp", None),
            P("dp", "ctx", None),
            P(owners),
            P(owners),
            P(owners, None, "mp"),
            P(None, "mp", owners),
            P("mp", owners),
            P(owners),
            P(owners, "mp"),
            P("mp", owners),
            P("mp", owners),
            P(owners),
        ),
        out_specs=(
            P("dp", "ctx", None),
            P("dp", "ctx", None),
            P(owners),
            P(owners),
            P(owners, None, "mp"),
            P(None, "mp", owners),
            P("mp", owners),
            P(owners),
            P(owners, "mp"),
            P("mp", owners),
            P("mp", owners),
            P(owners),
            P(),
        ),
        check_vma=False,
    )
```

```python
from functools import partial

import jax
import jax.numpy as jnp
import numpy as np
from jax import lax
from jax.experimental import pallas as pl
from jax.experimental.pallas import tpu as pltpu
from jax.sharding import PartitionSpec as P

HD = 64
ROT = 32
SEQ_LEN = 2048
PAIR = 2 * HD
TILE = 512

norm_eps = 1e-05
rotary_base = 10000.0
masked_fill = -1e30
low = jnp.bfloat16
wide = jnp.float32
gelu_in = (2.0 / 3.141592653589793) ** 0.5
gelu_cubic = 0.044715
vmem_limit = 48 * 1024 * 1024


def rotary_rows(seq):
    half = ROT // 2
    lane = np.arange(PAIR, dtype=np.int32)[None, :] % HD
    inverse = np.power(np.float32(rotary_base), -(lane % half).astype(np.float32) * np.float32(2.0 / ROT))
    angles = np.arange(seq, dtype=np.float32)[:, None] * inverse
    cosine, sine = np.cos(angles), np.sin(angles)
    return tuple(
        jnp.asarray(v.astype(np.float32))
        for v in (
            np.where(lane < ROT, cosine, 1.0),
            np.where(lane < half, -sine, 0.0),
            np.where((lane >= half) & (lane < ROT), sine, 0.0),
        )
    )


def attention_kernel(
    order_ref, qkv_ref, do_ref, cos_ref, up_ref, down_ref, mixed_ref, grad_ref,
    sorted_qkv, sorted_do, q_nat, k_nat, v_nat, do_nat, q_t, k_t, v_t, do_t,
    s_ref, dk_acc, dv_acc, out_s, grad_s, *, pieces, piece,
):
    blocks = pieces * piece // TILE
    scale = HD**-0.5
    dot = partial(jnp.dot, preferred_element_type=wide)

    def rows_of(b):
        return pl.ds(pl.multiple_of(b * TILE, TILE), TILE)

    def fold(t, how):
        return how(t.reshape(TILE // 8, 8, TILE), axis=0)

    def gather(r, _):
        src = pl.multiple_of(order_ref[r] * piece, piece)
        dst = pl.multiple_of(r * piece, piece)
        sorted_qkv[pl.ds(dst, piece), :] = qkv_ref[pl.ds(src, piece), :]
        sorted_do[pl.ds(dst, piece), :] = do_ref[pl.ds(src, piece), :]
        return 0

    lax.fori_loop(0, pieces, gather, 0)
    first = lax.broadcasted_iota(jnp.int32, (TILE, PAIR), 1) < HD

    def turn(t, rows, sign):
        up = pltpu.roll(t, PAIR - ROT // 2, 1) * up_ref[rows, :]
        down = pltpu.roll(t, ROT // 2, 1) * down_ref[rows, :]
        return t * cos_ref[rows, :] + sign * (up + down)

    def prepare(b, _):
        rows = rows_of(b)
        q = turn(sorted_qkv[rows, 0:PAIR], rows, 1.0).astype(low).astype(wide) * scale
        k = turn(sorted_qkv[rows, PAIR : 2 * PAIR], rows, 1.0)
        v = sorted_qkv[rows, 2 * PAIR : 3 * PAIR]
        g = sorted_do[rows, :].astype(wide)
        for val, nat, tr in ((q, q_nat, q_t), (k, k_nat, k_t), (v, v_nat, v_t), (g, do_nat, do_t)):
            nat[0, b] = jnp.where(first, val, 0.0).astype(low)
            nat[1, b] = jnp.where(first, 0.0, val).astype(low)
            tr[b] = val.T.astype(low)
        dk_acc[b] = jnp.zeros((TILE, PAIR), wide)
        dv_acc[b] = jnp.zeros((TILE, PAIR), wide)
        return 0

    for b in range(blocks):
        prepare(b, 0)
    key_row = lax.broadcasted_iota(jnp.int32, (TILE, TILE), 0)
    query_col = lax.broadcasted_iota(jnp.int32, (TILE, TILE), 1)
    allowed = key_row <= query_col

    def one_block(i, _):
        q_i = q_t[i]
        do_i = do_t[i]

        def score(j, tops):
            new = []
            for h in range(2):
                s = dot(k_nat[h, j], q_i)
                s_ref[h, j] = s
                new.append(jnp.maximum(tops[h], fold(s, jnp.max)))
            return tuple(new)

        partial_tops = (jnp.full((8, TILE), masked_fill, wide),) * 2
        for j in range(i):
            partial_tops = score(j, partial_tops)
        tops = []
        for h in range(2):
            s = jnp.where(allowed, dot(k_nat[h, i], q_i), masked_fill)
            s_ref[h, i] = s
            tops.append(
                jnp.max(jnp.maximum(partial_tops[h], fold(s, jnp.max)), axis=0, keepdims=True)
            )

        def weigh(j, carry):
            sums, accs = carry
            new_sums, new_accs = [], []
            for h in range(2):
                p = jnp.exp(s_ref[h, j] - tops[h])
                s_ref[h, j] = p
                new_sums.append(sums[h] + fold(p, jnp.sum))
                new_accs.append(accs[h] + dot(v_t[j, h * HD : (h + 1) * HD, :], p.astype(low)))
            return tuple(new_sums), tuple(new_accs)

        carry = ((jnp.zeros((8, TILE), wide),) * 2, (jnp.zeros((HD, TILE), wide),) * 2)
        for j in range(i + 1):
            carry = weigh(j, carry)
        sums, accs = carry
        invs, deltas, outs = [], [], []
        for h in range(2):
            inv = 1.0 / jnp.sum(sums[h], axis=0, keepdims=True)
            o = accs[h] * inv
            outs.append(o)
            invs.append(inv)
            g = do_i[h * HD : (h + 1) * HD, :].astype(wide)
            deltas.append(jnp.sum(o * g, axis=0, keepdims=True))
        out_s[i] = jnp.concatenate(outs, axis=0).T.astype(low)

        def pull(j, dq):
            new = []
            dv = dk = None
            for h in range(2):
                dp = dot(v_nat[h, j], do_i)
                p = s_ref[h, j] * invs[h]
                ds = (p * (dp - deltas[h])).astype(low)
                dv_h = dot(p.astype(low), do_nat[h, i])
                dk_h = dot(ds, q_nat[h, i])
                dv = dv_h if dv is None else dv + dv_h
                dk = dk_h if dk is None else dk + dk_h
                new.append(dq[h] + dot(k_t[j, h * HD : (h + 1) * HD, :], ds))
            dv_acc[j] += dv
            dk_acc[j] += dk
            return tuple(new)

        dq = (jnp.zeros((HD, TILE), wide),) * 2
        for j in range(i + 1):
            dq = pull(j, dq)
        rows = rows_of(i)
        dq_rows = jnp.concatenate(dq, axis=0).T * scale
        grad_s[rows, 0:PAIR] = turn(dq_rows, rows, -1.0).astype(low)
        return 0

    for b in range(blocks):
        one_block(b, 0)

    def finish(b, _):
        rows = rows_of(b)
        grad_s[rows, PAIR : 2 * PAIR] = turn(dk_acc[b], rows, -1.0).astype(low)
        grad_s[rows, 2 * PAIR : 3 * PAIR] = dv_acc[b].astype(low)
        sorted_do[rows, :] = out_s[b]
        return 0

    for b in range(blocks):
        finish(b, 0)

    def scatter(r, _):
        src = pl.multiple_of(order_ref[r] * piece, piece)
        dst = pl.multiple_of(r * piece, piece)
        mixed_ref[pl.ds(src, piece), :] = sorted_do[pl.ds(dst, piece), :]
        grad_ref[pl.ds(src, piece), :] = grad_s[pl.ds(dst, piece), :]
        return 0

    lax.fori_loop(0, pieces, scatter, 0)


def attention(order, qkv, grad_mixed, tables, deps):
    seq, width = grad_mixed.shape
    pairs = width // PAIR
    pieces = order.shape[0]
    blocks = seq // TILE
    vmem = pltpu.VMEM
    table = pl.BlockSpec((seq, PAIR), lambda p, o: (0, 0))
    one = pl.BlockSpec((seq, PAIR), lambda p, o: (0, p))
    three = pl.BlockSpec((seq, 3 * PAIR), lambda p, o: (0, p))
    kernel = partial(attention_kernel, pieces=pieces, piece=seq // pieces)
    count = len(deps)

    def inner(order_ref, *refs):
        kernel(order_ref, *refs[count:])

    return pl.pallas_call(
        inner,
        grid_spec=pltpu.PrefetchScalarGridSpec(
            num_scalar_prefetch=1,
            grid=(pairs,),
            in_specs=[pl.BlockSpec(memory_space=pl.ANY)] * count + [three, one, table, table, table],
            out_specs=[one, three],
            scratch_shapes=[
                vmem((seq, 3 * PAIR), wide),
                vmem((seq, PAIR), low),
                *[vmem((2, blocks, TILE, PAIR), low)] * 4,
                *[vmem((blocks, PAIR, TILE), low)] * 4,
                vmem((2, blocks, TILE, TILE), wide),
                vmem((blocks, TILE, PAIR), wide),
                vmem((blocks, TILE, PAIR), wide),
                vmem((blocks, TILE, PAIR), low),
                vmem((seq, 3 * PAIR), low),
            ],
        ),
        out_shape=[
            jax.ShapeDtypeStruct((seq, width), low),
            jax.ShapeDtypeStruct((seq, 3 * width), low),
        ],
        compiler_params=pltpu.CompilerParams(
            vmem_limit_bytes=48 * 1024 * 1024, dimension_semantics=("arbitrary",)
        ),
        cost_estimate=pl.CostEstimate(
            flops=pairs * 24 * seq * seq * PAIR, bytes_accessed=30_000_000, transcendentals=0
        ),
        name="attention",
    )(order, *deps, qkv, grad_mixed, *tables)


def call(body, name, grid, flags, in_specs, args, out_specs, out_shape, flops, moved, deps):
    count = len(deps)

    def inner(flag_ref, *refs):
        body(flag_ref, *refs[count:])

    in_specs = [pl.BlockSpec(memory_space=pl.ANY)] * count + in_specs
    args = [*deps, *args]
    return pl.pallas_call(
        inner,
        grid_spec=pltpu.PrefetchScalarGridSpec(
            num_scalar_prefetch=1, grid=grid, in_specs=in_specs, out_specs=out_specs
        ),
        out_shape=out_shape,
        compiler_params=pltpu.CompilerParams(vmem_limit_bytes=vmem_limit),
        cost_estimate=pl.CostEstimate(flops=flops, bytes_accessed=moved, transcendentals=0),
        name=name,
    )(flags, *args)


def quarter(n):
    return (n % 2) * 2 + n // 2


def product_nn(flags, a, chunks, width, kind, extra, deps):
    rows, model = a.shape
    fourth = model // 4
    step = min(rows, 512)
    count = len(chunks)

    def body(flag_ref, *refs):
        left = [ref[...] for ref in refs[:4]]
        outs = refs[4 + count + (extra is not None) :]
        for n in range(count):
            at = slice(n * width, (n + 1) * width)
            got = None
            for q in range(4):
                w = refs[4 + n][q * fourth : (q + 1) * fourth, :]
                one = jnp.dot(left[q], w, preferred_element_type=wide)
                got = one if got is None else got + one
            if kind == "plain":
                outs[0][:, at] = got.astype(low)
                continue
            more = refs[4 + count][:, at]
            if kind == "bias":
                outs[0][:, at] = got + more
            elif kind == "times":
                outs[0][:, at] = (got * more.astype(wide)).astype(low)
            else:
                v = got + more
                sq = v * v
                up = 0.5 + 0.5 * jnp.tanh(v * (gelu_in + gelu_in * gelu_cubic * sq))
                act = v * up
                outs[0][:, at] = act.astype(low)
                inner = 2.0 * gelu_in + 6.0 * gelu_in * gelu_cubic * sq
                outs[1][:, at] = (up + act * (1.0 - up) * inner).astype(low)

    total = count * width
    own = pl.BlockSpec((step, total), lambda i, f: (i, 0))
    in_specs = [
        pl.BlockSpec((step, fourth), partial(lambda col, i, f: (i, col), quarter(q)))
        for q in range(4)
    ]
    args = [a] * 4
    for weight, col in chunks:
        in_specs.append(pl.BlockSpec((model, width), partial(lambda col, i, f: (0, col), col)))
        args.append(weight)
    if kind == "times":
        extra, col = extra
        in_specs.append(pl.BlockSpec((step, total), lambda i, f: (i, col)))
        args.append(extra)
    elif extra is not None:
        in_specs.append(pl.BlockSpec((1, total), lambda i, f: (0, 0)))
        args.append(extra)
    outs = 2 if kind == "gelu" else 1
    out = call(
        body,
        "rows_" + kind,
        (rows // step,),
        flags,
        in_specs,
        args,
        [own] * outs,
        [jax.ShapeDtypeStruct((rows, total), wide if kind == "bias" else low)] * outs,
        2 * rows * model * total,
        2 * (rows * model + model * total + 2 * rows * total),
        deps,
    )
    return out if outs == 2 else out[0]


def product_tn(flags, outs, side, n_ctx, add, deps):
    rows, model = outs[0][0][0].shape
    half = model // 2
    step = half // 2
    d_own = step // n_ctx
    terms = [term for out in outs for term in out]
    count = len(terms)

    def body(flag_ref, *refs):
        n = 0
        for o, out in enumerate(outs):
            at = 0
            for _, _, _, width in out:
                got = lax.dot_general(
                    refs[n][...],
                    refs[count + n][...],
                    (((0,), (0,)), ((), ())),
                    preferred_element_type=wide,
                ).reshape(n_ctx, d_own, width)
                if add is not None:
                    got += refs[2 * count][:, 0, :, at : at + width].astype(wide)
                refs[-len(outs) + o][:, 0, :, at : at + width] = got.astype(low)
                n += 1
                at += width

    totals = [sum(term[3] for term in out) for out in outs]
    out_specs = [pl.BlockSpec((n_ctx, 1, d_own, t), lambda i, f: (0, i, 0, 0)) for t in totals]
    in_specs = [pl.BlockSpec((rows, step), lambda i, f: (0, 2 * (f[0] ^ side) + i))] * count
    in_specs += [
        pl.BlockSpec((rows, width), partial(lambda col, i, f: (0, col), col))
        for _, _, col, width in terms
    ]
    args = [term[0] for term in terms] + [term[1] for term in terms]
    if add is not None:
        in_specs.append(out_specs[0])
        args.append(add)
    return call(
        body,
        "weight_sums",
        (2,),
        flags,
        in_specs,
        args,
        out_specs,
        [jax.ShapeDtypeStruct((n_ctx, 2, d_own, t), low) for t in totals],
        2 * rows * half * sum(totals),
        2 * (rows * half * count + (rows + half) * sum(totals)),
        deps,
    )


def product_nt(flags, lefts, weights, cols, block, rows, add, split, deps):
    model = weights[0].shape[0]
    step = model // 4
    count = len(lefts)
    ks = [k for _, _, k in lefts]

    def body(flag_ref, *refs):
        got = None
        for a, w in zip(refs[:count], refs[count : 2 * count]):
            one = lax.dot_general(
                a[...], w[...], (((1,), (1,)), ((), ())), preferred_element_type=wide
            )
            got = one if got is None else got + one
        if add is not None:
            got += refs[2 * count][...].astype(wide)
        if split:
            refs[-2][...] = got[: rows // 2]
            refs[-1][...] = got[rows // 2 :].astype(low)
        else:
            refs[-1][...] = got.astype(low)

    in_specs = [
        pl.BlockSpec((rows, k), partial(lambda col, j, f: (block, col), col)) for _, col, k in lefts
    ]
    for (_, _, k), col in zip(lefts, cols):
        in_specs.append(pl.BlockSpec((step, k), partial(lambda col, j, f: (quarter(j), col), col)))
    args = [left for left, _, _ in lefts] + list(weights)
    if add is not None:
        in_specs.append(pl.BlockSpec((rows, step), lambda j, f: (0, j)))
        args.append(add)
    kept = rows // 2 if split else rows
    types = [wide, low] if split else [low]
    out = call(
        body,
        "feature_sums",
        (4,),
        flags,
        in_specs,
        args,
        [pl.BlockSpec((kept, step), lambda j, f: (0, j))] * len(types),
        [jax.ShapeDtypeStruct((kept, model), t) for t in types],
        2 * rows * model * sum(ks),
        2 * (rows + model) * sum(ks) + 4 * rows * model,
        deps,
    )
    return out if split else out[0]


def place_rows(flags, mine, other, n_seq, n_slot, base):
    model = mine.shape[1]
    part = n_slot // 4
    out_type = low if base is None else wide

    def body(flag_ref, *refs):
        own = pl.program_id(2) == flag_ref[1]

        @pl.when(own)
        def _():
            got = refs[0][...]
            refs[-1][...] = got if base is None else refs[2][...].astype(wide) + got.astype(wide)

        @pl.when(jnp.logical_not(own))
        def _():
            got = refs[1][...]
            refs[-1][...] = got if base is None else refs[2][...].astype(wide) + got.astype(wide)

    piece = pl.BlockSpec((part, model), lambda i, cc, yy, f: ((cc ^ f[0]) * n_seq + i, 0))
    slot = pl.BlockSpec((part, model), lambda i, cc, yy, f: (4 * i + 2 * cc + yy, 0))
    in_specs = [piece, piece]
    args = [mine, other]
    if base is not None:
        in_specs.append(slot)
        args.append(base.reshape(n_seq * n_slot, model))
    out = call(
        body,
        "place_rows",
        (n_seq, 2, 2),
        flags,
        in_specs,
        args,
        slot,
        jax.ShapeDtypeStruct((n_seq * n_slot, model), out_type),
        0,
        12 * n_seq * n_slot * model,
        [],
    )
    return out.reshape(n_seq, n_slot, model)


def stack_rows(flags, parts, deps):
    rows, model = parts[0].shape
    step = min(rows, 256)
    steps = rows // step

    def body(flag_ref, *refs):
        for n in range(len(parts)):

            @pl.when(pl.program_id(0) == n)
            def _():
                refs[-1][...] = refs[n][...]

    def at(n, i, j, f):
        return (jnp.where(i < n, 0, jnp.where(i > n, steps - 1, j)), 0)

    return call(
        body,
        "stack_rows",
        (len(parts), steps),
        flags,
        [pl.BlockSpec((step, model), partial(at, n)) for n in range(len(parts))],
        list(parts),
        pl.BlockSpec((step, model), lambda i, j, f: (i * steps + j, 0)),
        jax.ShapeDtypeStruct((len(parts) * rows, model), parts[0].dtype),
        0,
        4 * len(parts) * rows * model,
        deps,
    )


def never(*arrays):
    firsts = [v[(0,) * v.ndim] for v in arrays]
    return sum((v != v).astype(jnp.int32) for v in firsts)


def on_device(
    tokens,
    group_order,
    grad_out,
    norm_gain,
    norm_bias,
    w_qkv,
    b_qkv,
    w_out,
    b_out,
    w_fc1,
    b_fc1,
    w_fc2,
    b_fc2,
):
    n_dp = lax.axis_size("x") * lax.axis_size("core")
    n_ctx, n_mp = lax.axis_size("ctx"), lax.axis_size("mp")
    n_seq, n_slot, model = tokens.shape
    groups = group_order.shape[1]
    assert n_dp == 4 and 2 * n_seq == n_ctx == 4
    z, y = lax.axis_index("ctx"), lax.axis_index("mp")
    x, c = lax.axis_index("x"), lax.axis_index("core")
    dp = 2 * x + c
    half = model // 2
    part = n_slot // (2 * n_mp)
    rows_own = n_ctx * part
    block_len = SEQ_LEN // groups
    d_own = w_qkv.shape[0]
    flag_x = x.astype(jnp.int32).reshape(1)
    flag_cy = jnp.stack([c, y]).astype(jnp.int32)

    def to_core(v):
        return lax.ppermute(v, "core", [(0, 1), (1, 0)])

    def to_x(v):
        return lax.ppermute(v, "x", [(0, 1), (1, 0)])

    def to_z(v, k):
        return lax.ppermute(v, "ctx", [(i, i ^ k) for i in range(n_ctx)])

    def to_y(v):
        return lax.ppermute(v, "mp", [(0, 1), (1, 0)])

    def in_order(bit, mine, other, axis):
        return jnp.where(
            bit == 0,
            jnp.concatenate([mine, other], axis),
            jnp.concatenate([other, mine], axis),
        )

    def to_ctx(v):
        return lax.all_to_all(v, "ctx", 0, 0, tiled=True)

    def send_away(v, wait=0):
        cut = v.reshape(n_seq, 2, n_mp, part, model)

        def of_core(at):
            got = lax.dynamic_slice(
                cut, (0, at, y + wait, 0, 0), (n_seq, 1, 1, part, model)
            )
            return got.reshape(n_seq, part, model)

        return to_ctx(in_order(c, of_core(c), to_core(of_core(1 - c)), 0)).reshape(rows_own, model)

    def send_home(v):
        got = to_ctx(v.reshape(n_ctx, part, model))
        mine = lax.dynamic_slice_in_dim(got, n_seq * c, n_seq, 0)
        other = to_core(lax.dynamic_slice_in_dim(got, n_seq * (1 - c), n_seq, 0))
        homes = jnp.concatenate([mine, other], axis=0).reshape(rows_own, model)
        return homes, (to_y(homes) if n_mp == 2 else homes)

    def placed_home(homes, others, base=None):
        if n_mp == 2:
            return place_rows(flag_cy, homes, others, n_seq, n_slot, base)
        homes = lax.all_gather(homes.reshape(2, n_seq, part, model), "mp", axis=2, tiled=True)
        homes = jnp.where(c == 0, homes, homes[::-1])
        got = jnp.swapaxes(homes, 0, 1).reshape(n_seq, n_slot, model)
        return got if base is None else base.astype(wide) + got.astype(wide)

    def gather_rows(parts, deps_own, deps_all):
        if n_mp == 2:
            own = stack_rows(flag_x, [*parts, *[to_y(v) for v in parts]], deps_own)
        else:
            own = lax.all_gather(jnp.concatenate(parts, axis=0), "mp", axis=0, tiled=True)
        return stack_rows(flag_x, [own, to_core(own)], deps_all)

    small = jnp.concatenate(
        [norm_gain, norm_bias, b_out, b_fc2, b_qkv.reshape(-1), b_fc1.reshape(-1)]
    )
    small = jnp.pad(small, (0, -small.shape[0] % 128))[None]
    small = in_order(z % 2, small, to_z(small, 1), 0)
    small = in_order(z // 2, small, to_z(small, 2), 0)
    small = in_order(c, small, to_core(small), 0)
    small = in_order(x, small, to_x(small), 0)

    parts_in = send_away(tokens, never(small))

    pairs = w_qkv.shape[2] // PAIR // 2
    head_chunks = 2 if pairs % 2 == 0 else 1
    chunk_pairs = pairs // head_chunks
    qkv_cols = chunk_pairs * 3 * PAIR
    out_cols = chunk_pairs * PAIR
    hid = w_fc1.shape[1] // 2
    mlp_chunks = 2
    mlp_cols = hid // mlp_chunks
    qkv_split = w_qkv.reshape(d_own, 3, 2, head_chunks, chunk_pairs, PAIR).transpose(2, 3, 0, 4, 1, 5)
    qkv_split = qkv_split.reshape(2, head_chunks, d_own, qkv_cols)
    out_split = w_out.T.reshape(d_own, 2, head_chunks, out_cols).transpose(1, 2, 0, 3)
    heads_split = jnp.concatenate([qkv_split, out_split], axis=-1)
    fc1_split = w_fc1.reshape(d_own, 2, hid).transpose(1, 0, 2)
    fc2_split = w_fc2.T.reshape(d_own, 2, hid).transpose(1, 0, 2)

    def swap_cores(split):
        mine = lax.dynamic_index_in_dim(split, c, 0, keepdims=False)
        return mine, to_core(lax.dynamic_index_in_dim(split, 1 - c, 0, keepdims=False))

    def gather_weight(pair, at, width, wait=0):
        mine, other = (v[:, at : at + width] for v in pair)
        shard = in_order(c + wait, mine[None], other[None], 0)
        got = lax.all_gather(shard, ("x", "ctx"), axis=1, tiled=True)
        return got.reshape(model, width)

    first_cols = qkv_cols + out_cols
    heads_w = [gather_weight(swap_cores(heads_split[:, 0]), 0, first_cols)]
    more_split = jnp.concatenate([*(heads_split[:, n] for n in range(1, head_chunks)), fc1_split, fc2_split], axis=-1)
    more_pair = swap_cores(more_split)
    tokens_there = never(parts_in)
    parts_grad = send_away(grad_out, tokens_there)
    for n in range(1, head_chunks):
        heads_w.append(gather_weight(more_pair, (n - 1) * first_cols, first_cols, tokens_there))
    at = (head_chunks - 1) * first_cols
    fc1_w = gather_weight(more_pair, at, hid, tokens_there)
    fc2_w = gather_weight(more_pair, at + hid, hid, tokens_there)

    n_own = n_dp * n_ctx
    at = 0

    def take(count):
        nonlocal at
        got = small[:, at : at + count]
        at += count
        return got

    gain, shift, out_bias, fc2_bias = (take(d_own).reshape(model).astype(wide) for _ in range(4))
    heads_here, dims_here = b_qkv.shape[1:]
    qkv_bias = take(b_qkv.size).reshape(n_own, 3, heads_here, dims_here)
    qkv_bias = qkv_bias.transpose(1, 2, 0, 3).reshape(3, 2, head_chunks, chunk_pairs, PAIR)
    qkv_bias = lax.dynamic_index_in_dim(qkv_bias, c, 1, keepdims=False)
    qkv_bias = qkv_bias.transpose(1, 2, 0, 3).reshape(head_chunks, 1, qkv_cols).astype(wide)
    fc1_bias = take(b_fc1.size).reshape(n_own, b_fc1.shape[0], b_fc1.shape[1])
    fc1_bias = fc1_bias.transpose(1, 0, 2).reshape(2, 1, hid)
    fc1_bias = lax.dynamic_index_in_dim(fc1_bias, c, 0, keepdims=False).astype(wide)

    order_row = jnp.where(z // 2 == c, group_order, to_core(group_order))
    order_row = lax.dynamic_index_in_dim(order_row, z % 2, 0, keepdims=False)
    ids = jnp.arange(2 * n_mp * n_ctx, dtype=jnp.int32)
    at_core = (ids // (n_mp * n_ctx)) ^ c
    at_mp = (ids // n_ctx) % n_mp
    at_mp = at_mp ^ y if n_mp == 2 else at_mp
    at_ctx = ids % n_ctx
    slot = at_ctx * n_slot + at_core * (n_slot // 2) + at_mp * part
    chosen = (slot // block_len)[:, None] == jnp.arange(groups, dtype=jnp.int32)[None, :]
    block_at = jnp.sum(jnp.where(chosen, order_row[None, :], 0), axis=1)
    position = block_at * block_len + slot % block_len
    order = jnp.sum(jnp.where((position // part)[None, :] == ids[:, None], ids[None, :], 0), axis=1)
    tables = rotary_rows(SEQ_LEN)

    rows_in = parts_in.astype(wide)
    row_mean = jnp.mean(rows_in, axis=-1, keepdims=True)
    centered = rows_in - row_mean
    variance = jnp.mean(centered * centered, axis=-1, keepdims=True)
    inv_std = lax.rsqrt(variance + norm_eps)
    normed = centered * inv_std
    ln_out = gather_rows([(normed * gain + shift).astype(low)], [], [parts_grad])
    last = []

    def step(make, *deps):
        nonlocal last
        got = make([*last, *deps])
        last = [got[0] if isinstance(got, (tuple, list)) else got]
        return got

    def rows_step(a, chunks, width, kind, extra=None, deps=()):
        return step(lambda d: product_nn(flag_x, a, chunks, width, kind, extra, d), *deps)

    def far_sums(out, *deps):
        return out, to_x(step(lambda d: product_tn(flag_x, [out], 1, n_ctx, None, d), *deps)[0])

    def near_sums(far, *deps):
        out, came = far
        total = step(lambda d: product_tn(flag_x, [out], 0, n_ctx, came, d), *deps)[0]
        total = total.reshape(half, total.shape[-1])
        return lax.psum_scatter(total, "ctx", scatter_dimension=0, tiled=True)

    def feature_sums(lefts, weights, cols, *deps):
        rows = lefts[0][0].shape[0] // 2

        def run(block, add, split, more):
            return step(
                lambda d: product_nt(flag_x, lefts, weights, cols, block, rows, add, split, d), *more
            )

        came = to_core(run(1, None, False, deps))

        def two(*more):
            if n_mp == 2:
                mine, other = run(0, came, True, more)
                return mine, to_y(other)
            got = run(0, came, False, more)
            return lax.psum_scatter(got, "mp", scatter_dimension=0, tiled=True).astype(wide), None

        return two

    def joined(mine, came):
        return mine if came is None else mine + came.astype(wide)

    chunk_ids = range(head_chunks)
    both = range(mlp_chunks)
    qkv = [rows_step(ln_out, [(heads_w[0], 0)], qkv_cols, "bias", qkv_bias[0])]
    grad_rows = gather_rows([parts_grad], qkv, [])
    pulled = [rows_step(grad_rows, [(heads_w[0], 3)], out_cols, "plain")]
    for n in range(1, head_chunks):
        qkv.append(rows_step(ln_out, [(heads_w[n], 0)], qkv_cols, "bias", qkv_bias[n]))
        pulled.append(rows_step(grad_rows, [(heads_w[n], 3)], out_cols, "plain"))
    heads, heads_out, far_heads = [], [], []
    for n in chunk_ids:
        heads.append(step(lambda d: attention(order, qkv[n], pulled[n], tables, d)))
        mixed, grad_qkv = heads[n]
        heads_out.append([(ln_out, grad_qkv, 0, qkv_cols), (grad_rows, mixed, 0, out_cols)])
        far_heads.append(far_sums(heads_out[n]))
    act, slope = rows_step(ln_out, [(fc1_w, n) for n in both], mlp_cols, "gelu", fc1_bias)
    fc2_out = [[(grad_rows, act, n, mlp_cols)] for n in both]
    far_2a = far_sums(fc2_out[0], far_heads[0][1])
    attn_two = feature_sums([(h[0], 0, out_cols) for h in heads], heads_w, [3] * head_chunks)
    far_2b = far_sums(fc2_out[1])
    grad_heads = [near_sums(far_heads[0])]
    grad_pre = rows_step(
        grad_rows, [(fc2_w, n) for n in both], mlp_cols, "times", (slope, 0), (far_heads[-1][1],)
    )
    fc1_out = [[(ln_out, grad_pre, n, mlp_cols)] for n in both]
    far_1a = far_sums(fc1_out[0], far_2a[1])
    mlp_two = feature_sums([(act, 0, hid)], [fc2_w], [0])
    grad_heads += [near_sums(far) for far in far_heads[1:]]
    attn_mine, attn_came = attn_two()
    ln_two = feature_sums(
        [(grad_pre, 0, hid)] + [(h[1], 0, qkv_cols) for h in heads],
        [fc1_w, *heads_w],
        [0] * (1 + head_chunks),
    )
    mlp_mine, mlp_came = mlp_two()
    far_1b = far_sums(fc1_out[1], far_2b[1])
    grad_2 = [near_sums(far_2a, grad_heads[0])]
    grad_2.append(near_sums(far_2b))
    attn_out = joined(attn_mine, attn_came) + out_bias
    mlp_out = joined(mlp_mine, mlp_came) + fc2_bias
    block_rows = (rows_in + attn_out + mlp_out).astype(low)
    block_homes = send_home(block_rows)
    ln_mine, ln_came = ln_two(far_1a[1], block_rows)
    grad_1 = [near_sums(far_1a, grad_heads[-1], far_1b[1], block_homes[0])]
    grad_1.append(near_sums(far_1b, grad_2[0], block_homes[1]))

    grad_ln = ln_mine if ln_came is None else ln_mine + ln_came.astype(wide)
    scaled = grad_ln * gain
    back = inv_std * (
        scaled
        - jnp.mean(scaled, axis=-1, keepdims=True)
        - normed * jnp.mean(scaled * normed, axis=-1, keepdims=True)
    )
    back = back.astype(low)
    grad_homes = send_home(back)
    block_out = placed_home(*block_homes)
    grad_tokens = placed_home(*grad_homes, grad_out)
    gain_sum = jnp.sum(grad_ln * normed, axis=0)
    shift_sum = jnp.sum(grad_ln, axis=0)

    shared = jnp.concatenate(
        [
            gain_sum,
            shift_sum,
            jnp.sum(parts_grad.astype(wide), axis=0),
            jnp.stack(
                [
                    jnp.sum(rows_in * rows_in),
                    jnp.sum(attn_out * attn_out),
                    jnp.sum(mlp_out * mlp_out),
                ]
            ),
            jnp.zeros((125,), wide),
        ]
    )
    own = jnp.concatenate(
        [jnp.sum(v.astype(wide), axis=0) for v in [*(h[1] for h in heads), grad_pre]]
    )
    n_shared = shared.shape[0]
    sums = jnp.concatenate([shared, own])
    sums = sums + to_x(sums)
    sums = sums + to_z(sums, 1)
    sums = sums + to_z(sums, 2)
    if n_mp == 2:
        shared = sums[:n_shared]
        shared = shared + to_y(shared)
    else:
        shared = lax.psum(sums[:n_shared], "mp")
    sums = jnp.concatenate([shared, sums[n_shared:]])
    came = to_core(sums)
    shared = sums[:n_shared] + came[:n_shared]
    own = in_order(c, sums[None, n_shared:], came[None, n_shared:], 0)
    place = dp * n_ctx + z

    def own_slice(v):
        return lax.dynamic_slice_in_dim(v, place * d_own, d_own, 0)

    grad_gain = own_slice(shared[:model])
    grad_shift = own_slice(shared[model : 2 * model])
    grad_bias_out = own_slice(shared[2 * model : 3 * model])
    cells = n_dp * n_seq * SEQ_LEN * model
    root_means = jnp.sqrt(shared[3 * model : 3 * model + 3] / cells)
    n_heads = head_chunks * qkv_cols
    grad_b_qkv = own[:, :n_heads].reshape(2, pairs, 3, PAIR).transpose(2, 0, 1, 3)
    grad_b_qkv = grad_b_qkv.reshape(3, heads_here, HD)
    grad_b_qkv = lax.dynamic_slice_in_dim(grad_b_qkv, place * dims_here, dims_here, 2)
    grad_b_fc1 = own[:, n_heads:].reshape(b_fc1.shape[0], HD)
    grad_b_fc1 = lax.dynamic_slice_in_dim(grad_b_fc1, place * dims_here, dims_here, 1)

    def by_owner(parts):
        whole = jnp.stack([p.reshape(2, d_own, -1) for p in parts], axis=1)
        mine = lax.dynamic_index_in_dim(whole, c, 0, keepdims=True)
        other = to_core(lax.dynamic_index_in_dim(whole, 1 - c, 0, keepdims=True))
        return in_order(c, mine, other, 0)

    def join(v):
        return v.transpose(2, 0, 1, 3).reshape(d_own, -1).astype(wide)

    grad_h = by_owner(grad_heads)
    grad_w_qkv = grad_h[..., :qkv_cols].reshape(2, head_chunks, d_own, chunk_pairs, 3, PAIR)
    grad_w_qkv = grad_w_qkv.transpose(2, 4, 0, 1, 3, 5).reshape(d_own, 3, -1).astype(wide)
    grad_w_out = join(grad_h[..., qkv_cols:]).T
    return (
        block_out,
        grad_tokens,
        grad_gain,
        grad_shift,
        grad_w_qkv,
        grad_b_qkv,
        grad_w_out,
        grad_bias_out,
        join(by_owner(grad_1)),
        grad_b_fc1,
        join(by_owner(grad_2)).T,
        grad_bias_out,
        root_means,
    )


def solution(mesh):
    n_dp, n_ctx, n_mp = (mesh.shape[name] for name in ("dp", "ctx", "mp"))
    split = jax.sharding.Mesh(
        mesh.devices.reshape(n_dp // 2, 2, n_ctx, n_mp), ("x", "core", "ctx", "mp")
    )
    rows = ("x", "core")
    owners = ("x", "core", "ctx")
    return jax.shard_map(
        on_device,
        mesh=split,
        in_specs=(
            P(rows, "ctx", None),
            P(rows, None),
            P(rows, "ctx", None),
            P(owners),
            P(owners),
            P(owners, None, "mp"),
            P(None, "mp", owners),
            P("mp", owners),
            P(owners),
            P(owners, "mp"),
            P("mp", owners),
            P("mp", owners),
            P(owners),
        ),
        out_specs=(
            P(rows, "ctx", None),
            P(rows, "ctx", None),
            P(owners),
            P(owners),
            P(owners, None, "mp"),
            P(None, "mp", owners),
            P("mp", owners),
            P(owners),
            P(owners, "mp"),
            P("mp", owners),
            P("mp", owners),
            P(owners),
            P(),
        ),
        check_vma=False,
    )
```

```python
from functools import partial

import jax
import jax.numpy as jnp
import numpy as np
from jax import lax
from jax.experimental import pallas as pl
from jax.experimental.pallas import tpu as pltpu
from jax.sharding import PartitionSpec as P

HD = 64
ROT = 32
SEQ_LEN = 2048
PAIR = 2 * HD
TILE = 512

norm_eps = 1e-05
rotary_base = 10000.0
masked_fill = -1e30
low = jnp.bfloat16
wide = jnp.float32
gelu_in = (2.0 / 3.141592653589793) ** 0.5
gelu_cubic = 0.044715
vmem_limit = 48 * 1024 * 1024


def rotary_rows(seq):
    half = ROT // 2
    lane = np.arange(PAIR, dtype=np.int32)[None, :] % HD
    inverse = np.power(np.float32(rotary_base), -(lane % half).astype(np.float32) * np.float32(2.0 / ROT))
    angles = np.arange(seq, dtype=np.float32)[:, None] * inverse
    cosine, sine = np.cos(angles), np.sin(angles)
    return tuple(
        jnp.asarray(v.astype(np.float32))
        for v in (
            np.where(lane < ROT, cosine, 1.0),
            np.where(lane < half, -sine, 0.0),
            np.where((lane >= half) & (lane < ROT), sine, 0.0),
        )
    )


def attention_kernel(
    order_ref, qkv_ref, do_ref, cos_ref, up_ref, down_ref, mixed_ref, grad_ref,
    sorted_qkv, sorted_do, q_nat, k_nat, v_nat, do_nat, q_t, k_t, v_t, do_t,
    s_ref, dk_acc, dv_acc, out_s, grad_s, *, pieces, piece,
):
    blocks = pieces * piece // TILE
    scale = HD**-0.5
    dot = partial(jnp.dot, preferred_element_type=wide)

    def rows_of(b):
        return pl.ds(pl.multiple_of(b * TILE, TILE), TILE)

    def fold(t, how):
        return how(t.reshape(TILE // 8, 8, TILE), axis=0)

    def gather(r, _):
        src = pl.multiple_of(order_ref[r] * piece, piece)
        dst = pl.multiple_of(r * piece, piece)
        sorted_qkv[pl.ds(dst, piece), :] = qkv_ref[pl.ds(src, piece), :]
        sorted_do[pl.ds(dst, piece), :] = do_ref[pl.ds(src, piece), :]
        return 0

    lax.fori_loop(0, pieces, gather, 0)
    first = lax.broadcasted_iota(jnp.int32, (TILE, PAIR), 1) < HD

    def turn(t, rows, sign):
        up = pltpu.roll(t, PAIR - ROT // 2, 1) * up_ref[rows, :]
        down = pltpu.roll(t, ROT // 2, 1) * down_ref[rows, :]
        return t * cos_ref[rows, :] + sign * (up + down)

    def prepare(b, _):
        rows = rows_of(b)
        q = turn(sorted_qkv[rows, 0:PAIR], rows, 1.0).astype(low).astype(wide) * scale
        k = turn(sorted_qkv[rows, PAIR : 2 * PAIR], rows, 1.0)
        v = sorted_qkv[rows, 2 * PAIR : 3 * PAIR]
        g = sorted_do[rows, :].astype(wide)
        for val, nat, tr in ((q, q_nat, q_t), (k, k_nat, k_t), (v, v_nat, v_t), (g, do_nat, do_t)):
            nat[0, b] = jnp.where(first, val, 0.0).astype(low)
            nat[1, b] = jnp.where(first, 0.0, val).astype(low)
            tr[b] = val.T.astype(low)
        dk_acc[b] = jnp.zeros((TILE, PAIR), wide)
        dv_acc[b] = jnp.zeros((TILE, PAIR), wide)
        return 0

    for b in range(blocks):
        prepare(b, 0)
    key_row = lax.broadcasted_iota(jnp.int32, (TILE, TILE), 0)
    query_col = lax.broadcasted_iota(jnp.int32, (TILE, TILE), 1)
    allowed = key_row <= query_col

    def one_block(i, _):
        q_i = q_t[i]
        do_i = do_t[i]

        def score(j, tops):
            new = []
            for h in range(2):
                s = dot(k_nat[h, j], q_i)
                s_ref[h, j] = s
                new.append(jnp.maximum(tops[h], fold(s, jnp.max)))
            return tuple(new)

        partial_tops = (jnp.full((8, TILE), masked_fill, wide),) * 2
        for j in range(i):
            partial_tops = score(j, partial_tops)
        tops = []
        for h in range(2):
            s = jnp.where(allowed, dot(k_nat[h, i], q_i), masked_fill)
            s_ref[h, i] = s
            tops.append(
                jnp.max(jnp.maximum(partial_tops[h], fold(s, jnp.max)), axis=0, keepdims=True)
            )

        def weigh(j, carry):
            sums, accs = carry
            new_sums, new_accs = [], []
            for h in range(2):
                p = jnp.exp(s_ref[h, j] - tops[h])
                s_ref[h, j] = p
                new_sums.append(sums[h] + fold(p, jnp.sum))
                new_accs.append(accs[h] + dot(v_t[j, h * HD : (h + 1) * HD, :], p.astype(low)))
            return tuple(new_sums), tuple(new_accs)

        carry = ((jnp.zeros((8, TILE), wide),) * 2, (jnp.zeros((HD, TILE), wide),) * 2)
        for j in range(i + 1):
            carry = weigh(j, carry)
        sums, accs = carry
        invs, deltas, outs = [], [], []
        for h in range(2):
            inv = 1.0 / jnp.sum(sums[h], axis=0, keepdims=True)
            o = accs[h] * inv
            outs.append(o)
            invs.append(inv)
            g = do_i[h * HD : (h + 1) * HD, :].astype(wide)
            deltas.append(jnp.sum(o * g, axis=0, keepdims=True))
        out_s[i] = jnp.concatenate(outs, axis=0).T.astype(low)

        def pull(j, dq):
            new = []
            dv = dk = None
            for h in range(2):
                dp = dot(v_nat[h, j], do_i)
                p = s_ref[h, j] * invs[h]
                ds = (p * (dp - deltas[h])).astype(low)
                dv_h = dot(p.astype(low), do_nat[h, i])
                dk_h = dot(ds, q_nat[h, i])
                dv = dv_h if dv is None else dv + dv_h
                dk = dk_h if dk is None else dk + dk_h
                new.append(dq[h] + dot(k_t[j, h * HD : (h + 1) * HD, :], ds))
            dv_acc[j] += dv
            dk_acc[j] += dk
            return tuple(new)

        dq = (jnp.zeros((HD, TILE), wide),) * 2
        for j in range(i + 1):
            dq = pull(j, dq)
        rows = rows_of(i)
        dq_rows = jnp.concatenate(dq, axis=0).T * scale
        grad_s[rows, 0:PAIR] = turn(dq_rows, rows, -1.0).astype(low)
        return 0

    for b in range(blocks):
        one_block(b, 0)

    def finish(b, _):
        rows = rows_of(b)
        grad_s[rows, PAIR : 2 * PAIR] = turn(dk_acc[b], rows, -1.0).astype(low)
        grad_s[rows, 2 * PAIR : 3 * PAIR] = dv_acc[b].astype(low)
        sorted_do[rows, :] = out_s[b]
        return 0

    for b in range(blocks):
        finish(b, 0)

    def scatter(r, _):
        src = pl.multiple_of(order_ref[r] * piece, piece)
        dst = pl.multiple_of(r * piece, piece)
        mixed_ref[pl.ds(src, piece), :] = sorted_do[pl.ds(dst, piece), :]
        grad_ref[pl.ds(src, piece), :] = grad_s[pl.ds(dst, piece), :]
        return 0

    lax.fori_loop(0, pieces, scatter, 0)


def attention(order, qkv, grad_mixed, tables, deps):
    seq, width = grad_mixed.shape
    pairs = width // PAIR
    pieces = order.shape[0]
    blocks = seq // TILE
    vmem = pltpu.VMEM
    table = pl.BlockSpec((seq, PAIR), lambda p, o: (0, 0))
    one = pl.BlockSpec((seq, PAIR), lambda p, o: (0, p))
    three = pl.BlockSpec((seq, 3 * PAIR), lambda p, o: (0, p))
    kernel = partial(attention_kernel, pieces=pieces, piece=seq // pieces)
    count = len(deps)

    def inner(order_ref, *refs):
        kernel(order_ref, *refs[count:])

    return pl.pallas_call(
        inner,
        grid_spec=pltpu.PrefetchScalarGridSpec(
            num_scalar_prefetch=1,
            grid=(pairs,),
            in_specs=[pl.BlockSpec(memory_space=pl.ANY)] * count + [three, one, table, table, table],
            out_specs=[one, three],
            scratch_shapes=[
                vmem((seq, 3 * PAIR), wide),
                vmem((seq, PAIR), low),
                *[vmem((2, blocks, TILE, PAIR), low)] * 4,
                *[vmem((blocks, PAIR, TILE), low)] * 4,
                vmem((2, blocks, TILE, TILE), wide),
                vmem((blocks, TILE, PAIR), wide),
                vmem((blocks, TILE, PAIR), wide),
                vmem((blocks, TILE, PAIR), low),
                vmem((seq, 3 * PAIR), low),
            ],
        ),
        out_shape=[
            jax.ShapeDtypeStruct((seq, width), low),
            jax.ShapeDtypeStruct((seq, 3 * width), low),
        ],
        compiler_params=pltpu.CompilerParams(
            vmem_limit_bytes=48 * 1024 * 1024, dimension_semantics=("arbitrary",)
        ),
        cost_estimate=pl.CostEstimate(
            flops=pairs * 24 * seq * seq * PAIR, bytes_accessed=30_000_000, transcendentals=0
        ),
        name="attention",
    )(order, *deps, qkv, grad_mixed, *tables)


def call(body, name, grid, flags, in_specs, args, out_specs, out_shape, flops, moved, deps):
    count = len(deps)

    def inner(flag_ref, *refs):
        body(flag_ref, *refs[count:])

    in_specs = [pl.BlockSpec(memory_space=pl.ANY)] * count + in_specs
    args = [*deps, *args]
    return pl.pallas_call(
        inner,
        grid_spec=pltpu.PrefetchScalarGridSpec(
            num_scalar_prefetch=1, grid=grid, in_specs=in_specs, out_specs=out_specs
        ),
        out_shape=out_shape,
        compiler_params=pltpu.CompilerParams(vmem_limit_bytes=vmem_limit),
        cost_estimate=pl.CostEstimate(flops=flops, bytes_accessed=moved, transcendentals=0),
        name=name,
    )(flags, *args)


def quarter(n):
    return (n % 2) * 2 + n // 2


def product_nn(flags, a, chunks, width, kind, extra, deps):
    rows, model = a.shape
    fourth = model // 4
    step = min(rows, 512)
    count = len(chunks)

    def body(flag_ref, *refs):
        left = [ref[...] for ref in refs[:4]]
        outs = refs[4 + count + (extra is not None) :]
        for n in range(count):
            at = slice(n * width, (n + 1) * width)
            got = None
            for q in range(4):
                w = refs[4 + n][q * fourth : (q + 1) * fourth, :]
                one = jnp.dot(left[q], w, preferred_element_type=wide)
                got = one if got is None else got + one
            if kind == "plain":
                outs[0][:, at] = got.astype(low)
                continue
            more = refs[4 + count][:, at]
            if kind == "bias":
                outs[0][:, at] = got + more
            elif kind == "times":
                outs[0][:, at] = (got * more.astype(wide)).astype(low)
            else:
                v = got + more
                sq = v * v
                up = 0.5 + 0.5 * jnp.tanh(v * (gelu_in + gelu_in * gelu_cubic * sq))
                act = v * up
                outs[0][:, at] = act.astype(low)
                inner = 2.0 * gelu_in + 6.0 * gelu_in * gelu_cubic * sq
                outs[1][:, at] = (up + act * (1.0 - up) * inner).astype(low)

    total = count * width
    own = pl.BlockSpec((step, total), lambda i, f: (i, 0))
    in_specs = [
        pl.BlockSpec((step, fourth), partial(lambda col, i, f: (i, col), quarter(q)))
        for q in range(4)
    ]
    args = [a] * 4
    for weight, col in chunks:
        in_specs.append(pl.BlockSpec((model, width), partial(lambda col, i, f: (0, col), col)))
        args.append(weight)
    if kind == "times":
        extra, col = extra
        in_specs.append(pl.BlockSpec((step, total), lambda i, f: (i, col)))
        args.append(extra)
    elif extra is not None:
        in_specs.append(pl.BlockSpec((1, total), lambda i, f: (0, 0)))
        args.append(extra)
    outs = 2 if kind == "gelu" else 1
    out = call(
        body,
        "rows_" + kind,
        (rows // step,),
        flags,
        in_specs,
        args,
        [own] * outs,
        [jax.ShapeDtypeStruct((rows, total), wide if kind == "bias" else low)] * outs,
        2 * rows * model * total,
        2 * (rows * model + model * total + 2 * rows * total),
        deps,
    )
    return out if outs == 2 else out[0]


def product_tn(flags, outs, side, n_ctx, add, deps):
    rows, model = outs[0][0][0].shape
    half = model // 2
    step = half // 2
    d_own = step // n_ctx
    terms = [term for out in outs for term in out]
    count = len(terms)

    def body(flag_ref, *refs):
        n = 0
        for o, out in enumerate(outs):
            at = 0
            for _, _, _, width in out:
                got = lax.dot_general(
                    refs[n][...],
                    refs[count + n][...],
                    (((0,), (0,)), ((), ())),
                    preferred_element_type=wide,
                ).reshape(n_ctx, d_own, width)
                if add is not None:
                    got += refs[2 * count][:, 0, :, at : at + width].astype(wide)
                refs[-len(outs) + o][:, 0, :, at : at + width] = got.astype(low)
                n += 1
                at += width

    totals = [sum(term[3] for term in out) for out in outs]
    out_specs = [pl.BlockSpec((n_ctx, 1, d_own, t), lambda i, f: (0, i, 0, 0)) for t in totals]
    in_specs = [pl.BlockSpec((rows, step), lambda i, f: (0, 2 * (f[0] ^ side) + i))] * count
    in_specs += [
        pl.BlockSpec((rows, width), partial(lambda col, i, f: (0, col), col))
        for _, _, col, width in terms
    ]
    args = [term[0] for term in terms] + [term[1] for term in terms]
    if add is not None:
        in_specs.append(out_specs[0])
        args.append(add)
    return call(
        body,
        "weight_sums",
        (2,),
        flags,
        in_specs,
        args,
        out_specs,
        [jax.ShapeDtypeStruct((n_ctx, 2, d_own, t), low) for t in totals],
        2 * rows * half * sum(totals),
        2 * (rows * half * count + (rows + half) * sum(totals)),
        deps,
    )


def product_nt(flags, lefts, weights, cols, block, rows, add, split, deps):
    model = weights[0].shape[0]
    step = model // 4
    count = len(lefts)
    ks = [k for _, _, k in lefts]

    def body(flag_ref, *refs):
        got = None
        for a, w in zip(refs[:count], refs[count : 2 * count]):
            one = lax.dot_general(
                a[...], w[...], (((1,), (1,)), ((), ())), preferred_element_type=wide
            )
            got = one if got is None else got + one
        if add is not None:
            got += refs[2 * count][...].astype(wide)
        if split:
            refs[-2][...] = got[: rows // 2]
            refs[-1][...] = got[rows // 2 :].astype(low)
        else:
            refs[-1][...] = got.astype(low)

    in_specs = [
        pl.BlockSpec((rows, k), partial(lambda col, j, f: (block, col), col)) for _, col, k in lefts
    ]
    for (_, _, k), col in zip(lefts, cols):
        in_specs.append(pl.BlockSpec((step, k), partial(lambda col, j, f: (quarter(j), col), col)))
    args = [left for left, _, _ in lefts] + list(weights)
    if add is not None:
        in_specs.append(pl.BlockSpec((rows, step), lambda j, f: (0, j)))
        args.append(add)
    kept = rows // 2 if split else rows
    types = [wide, low] if split else [low]
    out = call(
        body,
        "feature_sums",
        (4,),
        flags,
        in_specs,
        args,
        [pl.BlockSpec((kept, step), lambda j, f: (0, j))] * len(types),
        [jax.ShapeDtypeStruct((kept, model), t) for t in types],
        2 * rows * model * sum(ks),
        2 * (rows + model) * sum(ks) + 4 * rows * model,
        deps,
    )
    return out if split else out[0]


def place_rows(flags, mine, mine_y, came, n_seq, n_slot, base):
    model = mine.shape[1]
    part = n_slot // 4
    out_type = low if base is None else wide

    def body(flag_ref, *refs):
        own_core = pl.program_id(1) == flag_ref[0]
        own_mp = pl.program_id(2) == flag_ref[1]

        def put(ref):
            got = ref[...]
            refs[-1][...] = got if base is None else refs[3][...].astype(wide) + got.astype(wide)

        @pl.when(own_core & own_mp)
        def _():
            put(refs[0])

        @pl.when(own_core & jnp.logical_not(own_mp))
        def _():
            put(refs[1])

        @pl.when(jnp.logical_not(own_core))
        def _():
            put(refs[2])

    piece = pl.BlockSpec((part, model), lambda i, cc, yy, f: (n_seq * f[0] + i, 0))
    other = pl.BlockSpec((part, model), lambda i, cc, yy, f: (n_seq * (yy ^ f[1]) + i, 0))
    slot = pl.BlockSpec((part, model), lambda i, cc, yy, f: (4 * i + 2 * cc + yy, 0))
    in_specs = [piece, piece, other]
    args = [mine, mine_y, came]
    if base is not None:
        in_specs.append(slot)
        args.append(base.reshape(n_seq * n_slot, model))
    out = call(
        body,
        "place_rows",
        (n_seq, 2, 2),
        flags,
        in_specs,
        args,
        slot,
        jax.ShapeDtypeStruct((n_seq * n_slot, model), out_type),
        0,
        12 * n_seq * n_slot * model,
        [],
    )
    return out.reshape(n_seq, n_slot, model)


def stack_rows(flags, parts, deps):
    rows, model = parts[0].shape
    step = min(rows, 256)
    steps = rows // step

    def body(flag_ref, *refs):
        for n in range(len(parts)):

            @pl.when(pl.program_id(0) == n)
            def _():
                refs[-1][...] = refs[n][...]

    def at(n, i, j, f):
        return (jnp.where(i < n, 0, jnp.where(i > n, steps - 1, j)), 0)

    return call(
        body,
        "stack_rows",
        (len(parts), steps),
        flags,
        [pl.BlockSpec((step, model), partial(at, n)) for n in range(len(parts))],
        list(parts),
        pl.BlockSpec((step, model), lambda i, j, f: (i * steps + j, 0)),
        jax.ShapeDtypeStruct((len(parts) * rows, model), parts[0].dtype),
        0,
        4 * len(parts) * rows * model,
        deps,
    )


def never(*arrays):
    firsts = [v[(0,) * v.ndim] for v in arrays]
    return sum((v != v).astype(jnp.int32) for v in firsts)


def on_device(
    tokens,
    group_order,
    grad_out,
    norm_gain,
    norm_bias,
    w_qkv,
    b_qkv,
    w_out,
    b_out,
    w_fc1,
    b_fc1,
    w_fc2,
    b_fc2,
):
    n_dp = lax.axis_size("x") * lax.axis_size("core")
    n_ctx, n_mp = lax.axis_size("ctx"), lax.axis_size("mp")
    n_seq, n_slot, model = tokens.shape
    groups = group_order.shape[1]
    assert n_dp == 4 and 2 * n_seq == n_ctx == 4
    z, y = lax.axis_index("ctx"), lax.axis_index("mp")
    x, c = lax.axis_index("x"), lax.axis_index("core")
    dp = 2 * x + c
    half = model // 2
    part = n_slot // (2 * n_mp)
    rows_own = n_ctx * part
    block_len = SEQ_LEN // groups
    d_own = w_qkv.shape[0]
    flag_x = x.astype(jnp.int32).reshape(1)
    flag_cy = jnp.stack([c, y]).astype(jnp.int32)

    def to_core(v):
        return lax.ppermute(v, "core", [(0, 1), (1, 0)])

    def to_x(v):
        return lax.ppermute(v, "x", [(0, 1), (1, 0)])

    def to_z(v, k):
        return lax.ppermute(v, "ctx", [(i, i ^ k) for i in range(n_ctx)])

    def to_y(v):
        return lax.ppermute(v, "mp", [(0, 1), (1, 0)])

    def in_order(bit, mine, other, axis):
        return jnp.where(
            bit == 0,
            jnp.concatenate([mine, other], axis),
            jnp.concatenate([other, mine], axis),
        )

    def to_ctx(v):
        return lax.all_to_all(v, "ctx", 0, 0, tiled=True)

    def send_away(v, wait=0):
        cut = v.reshape(n_seq, 2, n_mp, part, model)

        def of_core(at):
            got = lax.dynamic_slice(
                cut, (0, at, y + wait, 0, 0), (n_seq, 1, 1, part, model)
            )
            return got.reshape(n_seq, part, model)

        return to_ctx(in_order(c, of_core(c), to_core(of_core(1 - c)), 0)).reshape(rows_own, model)

    def send_home(v):
        return to_ctx(v.reshape(n_ctx, part, model))

    def other_mp(got, wait=0):
        return to_y(got + jnp.asarray(wait, got.dtype)) if n_mp == 2 else got

    def placed_home(got, got_y, base=None):
        def of_core(at):
            return [lax.dynamic_slice_in_dim(v, n_seq * at, n_seq, 0) for v in (got, got_y)]

        if n_mp == 2:
            came = to_core(jnp.concatenate(of_core(1 - c), axis=0))
            flat = [v.reshape(rows_own, model) for v in (got, got_y, came)]
            return place_rows(flag_cy, *flat, n_seq, n_slot, base)
        mine = lax.all_gather(of_core(c)[0], "mp", axis=1, tiled=True)
        other = to_core(lax.all_gather(of_core(1 - c)[0], "mp", axis=1, tiled=True))
        got = jnp.where(c == 0, jnp.stack([mine, other]), jnp.stack([other, mine]))
        got = jnp.swapaxes(got, 0, 1).reshape(n_seq, n_slot, model)
        return got if base is None else base.astype(wide) + got.astype(wide)

    def gather_rows(parts, deps_own, deps_all):
        if n_mp == 2:
            own = stack_rows(flag_x, [*parts, *[to_y(v) for v in parts]], deps_own)
        else:
            own = lax.all_gather(jnp.concatenate(parts, axis=0), "mp", axis=0, tiled=True)
        return stack_rows(flag_x, [own, to_core(own)], deps_all)

    small = jnp.concatenate(
        [norm_gain, norm_bias, b_out, b_fc2, b_qkv.reshape(-1), b_fc1.reshape(-1)]
    )
    small = jnp.pad(small, (0, -small.shape[0] % 128))[None]
    small = in_order(z % 2, small, to_z(small, 1), 0)
    small = in_order(z // 2, small, to_z(small, 2), 0)
    small = in_order(c, small, to_core(small), 0)
    small = in_order(x, small, to_x(small), 0)

    parts_in = send_away(tokens, never(small))

    pairs = w_qkv.shape[2] // PAIR // 2
    head_chunks = 2 if pairs % 2 == 0 else 1
    chunk_pairs = pairs // head_chunks
    qkv_cols = chunk_pairs * 3 * PAIR
    out_cols = chunk_pairs * PAIR
    hid = w_fc1.shape[1] // 2
    mlp_chunks = 2
    mlp_cols = hid // mlp_chunks
    qkv_split = w_qkv.reshape(d_own, 3, 2, head_chunks, chunk_pairs, PAIR).transpose(2, 3, 0, 4, 1, 5)
    qkv_split = qkv_split.reshape(2, head_chunks, d_own, qkv_cols)
    out_split = w_out.T.reshape(d_own, 2, head_chunks, out_cols).transpose(1, 2, 0, 3)
    heads_split = jnp.concatenate([qkv_split, out_split], axis=-1)
    fc1_split = w_fc1.reshape(d_own, 2, hid).transpose(1, 0, 2)
    fc2_split = w_fc2.T.reshape(d_own, 2, hid).transpose(1, 0, 2)

    def swap_cores(split):
        mine = lax.dynamic_index_in_dim(split, c, 0, keepdims=False)
        return mine, to_core(lax.dynamic_index_in_dim(split, 1 - c, 0, keepdims=False))

    def gather_weight(pair, at, width, wait=0):
        mine, other = (v[:, at : at + width] for v in pair)
        shard = in_order(c + wait, mine[None], other[None], 0)
        got = lax.all_gather(shard, ("x", "ctx"), axis=1, tiled=True)
        return got.reshape(model, width)

    first_cols = qkv_cols + out_cols
    heads_w = [gather_weight(swap_cores(heads_split[:, 0]), 0, first_cols)]
    more_split = jnp.concatenate([*(heads_split[:, n] for n in range(1, head_chunks)), fc1_split, fc2_split], axis=-1)
    more_pair = swap_cores(more_split)
    tokens_there = never(parts_in)
    parts_grad = send_away(grad_out, tokens_there)
    for n in range(1, head_chunks):
        heads_w.append(gather_weight(more_pair, (n - 1) * first_cols, first_cols, tokens_there))
    at = (head_chunks - 1) * first_cols
    fc1_w = gather_weight(more_pair, at, hid, tokens_there)
    fc2_w = gather_weight(more_pair, at + hid, hid, tokens_there)

    n_own = n_dp * n_ctx
    at = 0

    def take(count):
        nonlocal at
        got = small[:, at : at + count]
        at += count
        return got

    gain, shift, out_bias, fc2_bias = (take(d_own).reshape(model).astype(wide) for _ in range(4))
    heads_here, dims_here = b_qkv.shape[1:]
    qkv_bias = take(b_qkv.size).reshape(n_own, 3, heads_here, dims_here)
    qkv_bias = qkv_bias.transpose(1, 2, 0, 3).reshape(3, 2, head_chunks, chunk_pairs, PAIR)
    qkv_bias = lax.dynamic_index_in_dim(qkv_bias, c, 1, keepdims=False)
    qkv_bias = qkv_bias.transpose(1, 2, 0, 3).reshape(head_chunks, 1, qkv_cols).astype(wide)
    fc1_bias = take(b_fc1.size).reshape(n_own, b_fc1.shape[0], b_fc1.shape[1])
    fc1_bias = fc1_bias.transpose(1, 0, 2).reshape(2, 1, hid)
    fc1_bias = lax.dynamic_index_in_dim(fc1_bias, c, 0, keepdims=False).astype(wide)

    order_row = jnp.where(z // 2 == c, group_order, to_core(group_order))
    order_row = lax.dynamic_index_in_dim(order_row, z % 2, 0, keepdims=False)
    ids = jnp.arange(2 * n_mp * n_ctx, dtype=jnp.int32)
    at_core = (ids // (n_mp * n_ctx)) ^ c
    at_mp = (ids // n_ctx) % n_mp
    at_mp = at_mp ^ y if n_mp == 2 else at_mp
    at_ctx = ids % n_ctx
    slot = at_ctx * n_slot + at_core * (n_slot // 2) + at_mp * part
    chosen = (slot // block_len)[:, None] == jnp.arange(groups, dtype=jnp.int32)[None, :]
    block_at = jnp.sum(jnp.where(chosen, order_row[None, :], 0), axis=1)
    position = block_at * block_len + slot % block_len
    order = jnp.sum(jnp.where((position // part)[None, :] == ids[:, None], ids[None, :], 0), axis=1)
    tables = rotary_rows(SEQ_LEN)

    rows_in = parts_in.astype(wide)
    row_mean = jnp.mean(rows_in, axis=-1, keepdims=True)
    centered = rows_in - row_mean
    variance = jnp.mean(centered * centered, axis=-1, keepdims=True)
    inv_std = lax.rsqrt(variance + norm_eps)
    normed = centered * inv_std
    ln_out = gather_rows([(normed * gain + shift).astype(low)], [], [parts_grad])
    last = []

    def step(make, *deps):
        nonlocal last
        got = make([*last, *deps])
        last = [got[0] if isinstance(got, (tuple, list)) else got]
        return got

    def rows_step(a, chunks, width, kind, extra=None, deps=()):
        return step(lambda d: product_nn(flag_x, a, chunks, width, kind, extra, d), *deps)

    def far_sums(out, *deps):
        return out, to_x(step(lambda d: product_tn(flag_x, [out], 1, n_ctx, None, d), *deps)[0])

    def near_sums(far, *deps):
        out, came = far
        total = step(lambda d: product_tn(flag_x, [out], 0, n_ctx, came, d), *deps)[0]
        total = total.reshape(half, total.shape[-1])
        return lax.psum_scatter(total, "ctx", scatter_dimension=0, tiled=True)

    def feature_sums(lefts, weights, cols, *deps):
        rows = lefts[0][0].shape[0] // 2

        def run(block, add, split, more):
            return step(
                lambda d: product_nt(flag_x, lefts, weights, cols, block, rows, add, split, d), *more
            )

        came = to_core(run(1, None, False, deps))

        def two(*more):
            if n_mp == 2:
                mine, other = run(0, came, True, more)
                return mine, to_y(other)
            got = run(0, came, False, more)
            return lax.psum_scatter(got, "mp", scatter_dimension=0, tiled=True).astype(wide), None

        return two

    def joined(mine, came):
        return mine if came is None else mine + came.astype(wide)

    chunk_ids = range(head_chunks)
    both = range(mlp_chunks)
    qkv = [rows_step(ln_out, [(heads_w[0], 0)], qkv_cols, "bias", qkv_bias[0])]
    grad_rows = gather_rows([parts_grad], qkv, [])
    pulled = [rows_step(grad_rows, [(heads_w[0], 3)], out_cols, "plain")]
    for n in range(1, head_chunks):
        qkv.append(rows_step(ln_out, [(heads_w[n], 0)], qkv_cols, "bias", qkv_bias[n]))
        pulled.append(rows_step(grad_rows, [(heads_w[n], 3)], out_cols, "plain"))
    heads, heads_out, far_heads = [], [], []
    for n in chunk_ids:
        heads.append(step(lambda d: attention(order, qkv[n], pulled[n], tables, d)))
        mixed, grad_qkv = heads[n]
        heads_out.append([(ln_out, grad_qkv, 0, qkv_cols), (grad_rows, mixed, 0, out_cols)])
        far_heads.append(far_sums(heads_out[n]))
    act, slope = rows_step(ln_out, [(fc1_w, n) for n in both], mlp_cols, "gelu", fc1_bias)
    fc2_out = [[(grad_rows, act, n, mlp_cols)] for n in both]
    far_2a = far_sums(fc2_out[0], far_heads[0][1])
    attn_two = feature_sums([(h[0], 0, out_cols) for h in heads], heads_w, [3] * head_chunks)
    far_2b = far_sums(fc2_out[1])
    grad_heads = [near_sums(far_heads[0])]
    attn_mine, attn_came = attn_two()
    mlp_two = feature_sums([(act, 0, hid)], [fc2_w], [0], far_heads[-1][1])
    grad_heads += [near_sums(far) for far in far_heads[1:]]
    mlp_mine, mlp_came = mlp_two()
    grad_pre = rows_step(grad_rows, [(fc2_w, n) for n in both], mlp_cols, "times", (slope, 0))
    fc1_out = [[(ln_out, grad_pre, n, mlp_cols)] for n in both]
    far_1a = far_sums(fc1_out[0], far_2a[1])
    ln_two = feature_sums(
        [(grad_pre, 0, hid)] + [(h[1], 0, qkv_cols) for h in heads],
        [fc1_w, *heads_w],
        [0] * (1 + head_chunks),
        *([] if attn_came is None else [attn_came]),
    )
    far_1b = far_sums(fc1_out[1], far_2b[1])
    attn_out = joined(attn_mine, attn_came) + out_bias
    mlp_out = joined(mlp_mine, mlp_came) + fc2_bias
    block_rows = (rows_in + attn_out + mlp_out).astype(low)
    block_got = send_home(block_rows)
    grad_2 = [near_sums(far_2a, grad_heads[0], block_rows)]
    grad_2.append(near_sums(far_2b))
    ln_mine, ln_came = ln_two(far_1a[1], block_got)
    grad_1 = [near_sums(far_1a, grad_heads[-1], far_1b[1])]
    block_y = other_mp(block_got, 0 if ln_came is None else never(ln_came))
    grad_1.append(near_sums(far_1b, grad_2[0], block_y))

    grad_ln = ln_mine if ln_came is None else ln_mine + ln_came.astype(wide)
    scaled = grad_ln * gain
    back = inv_std * (
        scaled
        - jnp.mean(scaled, axis=-1, keepdims=True)
        - normed * jnp.mean(scaled * normed, axis=-1, keepdims=True)
    )
    back = back.astype(low)
    grad_got = send_home(back)
    block_out = placed_home(block_got, block_y)
    grad_tokens = placed_home(grad_got, other_mp(grad_got), grad_out)
    gain_sum = jnp.sum(grad_ln * normed, axis=0)
    shift_sum = jnp.sum(grad_ln, axis=0)

    shared = jnp.concatenate(
        [
            gain_sum,
            shift_sum,
            jnp.sum(parts_grad.astype(wide), axis=0),
            jnp.stack(
                [
                    jnp.sum(rows_in * rows_in),
                    jnp.sum(attn_out * attn_out),
                    jnp.sum(mlp_out * mlp_out),
                ]
            ),
            jnp.zeros((125,), wide),
        ]
    )
    own = jnp.concatenate(
        [jnp.sum(v.astype(wide), axis=0) for v in [*(h[1] for h in heads), grad_pre]]
    )
    n_shared = shared.shape[0]
    sums = jnp.concatenate([shared, own])
    sums = sums + to_x(sums)
    sums = sums + to_z(sums, 1)
    sums = sums + to_z(sums, 2)
    if n_mp == 2:
        shared = sums[:n_shared]
        shared = shared + to_y(shared)
    else:
        shared = lax.psum(sums[:n_shared], "mp")
    sums = jnp.concatenate([shared, sums[n_shared:]])
    came = to_core(sums)
    shared = sums[:n_shared] + came[:n_shared]
    own = in_order(c, sums[None, n_shared:], came[None, n_shared:], 0)
    place = dp * n_ctx + z

    def own_slice(v):
        return lax.dynamic_slice_in_dim(v, place * d_own, d_own, 0)

    grad_gain = own_slice(shared[:model])
    grad_shift = own_slice(shared[model : 2 * model])
    grad_bias_out = own_slice(shared[2 * model : 3 * model])
    cells = n_dp * n_seq * SEQ_LEN * model
    root_means = jnp.sqrt(shared[3 * model : 3 * model + 3] / cells)
    n_heads = head_chunks * qkv_cols
    grad_b_qkv = own[:, :n_heads].reshape(2, pairs, 3, PAIR).transpose(2, 0, 1, 3)
    grad_b_qkv = grad_b_qkv.reshape(3, heads_here, HD)
    grad_b_qkv = lax.dynamic_slice_in_dim(grad_b_qkv, place * dims_here, dims_here, 2)
    grad_b_fc1 = own[:, n_heads:].reshape(b_fc1.shape[0], HD)
    grad_b_fc1 = lax.dynamic_slice_in_dim(grad_b_fc1, place * dims_here, dims_here, 1)

    def by_owner(parts):
        whole = jnp.stack([p.reshape(2, d_own, -1) for p in parts], axis=1)
        mine = lax.dynamic_index_in_dim(whole, c, 0, keepdims=True)
        other = to_core(lax.dynamic_index_in_dim(whole, 1 - c, 0, keepdims=True))
        return in_order(c, mine, other, 0)

    def join(v):
        return v.transpose(2, 0, 1, 3).reshape(d_own, -1).astype(wide)

    grad_h = by_owner(grad_heads)
    grad_w_qkv = grad_h[..., :qkv_cols].reshape(2, head_chunks, d_own, chunk_pairs, 3, PAIR)
    grad_w_qkv = grad_w_qkv.transpose(2, 4, 0, 1, 3, 5).reshape(d_own, 3, -1).astype(wide)
    grad_w_out = join(grad_h[..., qkv_cols:]).T
    return (
        block_out,
        grad_tokens,
        grad_gain,
        grad_shift,
        grad_w_qkv,
        grad_b_qkv,
        grad_w_out,
        grad_bias_out,
        join(by_owner(grad_1)),
        grad_b_fc1,
        join(by_owner(grad_2)).T,
        grad_bias_out,
        root_means,
    )


def solution(mesh):
    n_dp, n_ctx, n_mp = (mesh.shape[name] for name in ("dp", "ctx", "mp"))
    split = jax.sharding.Mesh(
        mesh.devices.reshape(n_dp // 2, 2, n_ctx, n_mp), ("x", "core", "ctx", "mp")
    )
    rows = ("x", "core")
    owners = ("x", "core", "ctx")
    return jax.shard_map(
        on_device,
        mesh=split,
        in_specs=(
            P(rows, "ctx", None),
            P(rows, None),
            P(rows, "ctx", None),
            P(owners),
            P(owners),
            P(owners, None, "mp"),
            P(None, "mp", owners),
            P("mp", owners),
            P(owners),
            P(owners, "mp"),
            P("mp", owners),
            P("mp", owners),
            P(owners),
        ),
        out_specs=(
            P(rows, "ctx", None),
            P(rows, "ctx", None),
            P(owners),
            P(owners),
            P(owners, None, "mp"),
            P(None, "mp", owners),
            P("mp", owners),
            P(owners),
            P(owners, "mp"),
            P("mp", owners),
            P("mp", owners),
            P(owners),
            P(),
        ),
        check_vma=False,
    )
```

```python
from functools import partial

import jax
import jax.numpy as jnp
import numpy as np
from jax import lax
from jax.experimental import pallas as pl
from jax.experimental.pallas import tpu as pltpu
from jax.sharding import PartitionSpec as P

HD = 64
ROT = 32
SEQ_LEN = 2048
PAIR = 2 * HD
TILE = 512

norm_eps = 1e-05
rotary_base = 10000.0
masked_fill = -1e30
low = jnp.bfloat16
wide = jnp.float32
gelu_in = (2.0 / 3.141592653589793) ** 0.5
gelu_cubic = 0.044715
vmem_limit = 48 * 1024 * 1024


def rotary_rows(seq):
    half = ROT // 2
    lane = np.arange(PAIR, dtype=np.int32)[None, :] % HD
    inverse = np.power(np.float32(rotary_base), -(lane % half).astype(np.float32) * np.float32(2.0 / ROT))
    angles = np.arange(seq, dtype=np.float32)[:, None] * inverse
    cosine, sine = np.cos(angles), np.sin(angles)
    return tuple(
        jnp.asarray(v.astype(np.float32))
        for v in (
            np.where(lane < ROT, cosine, 1.0),
            np.where(lane < half, -sine, 0.0),
            np.where((lane >= half) & (lane < ROT), sine, 0.0),
        )
    )


def attention_kernel(
    order_ref, qkv_ref, do_ref, cos_ref, up_ref, down_ref, mixed_ref, grad_ref,
    sorted_qkv, sorted_do, q_nat, k_nat, v_nat, do_nat, q_t, k_t, v_t, do_t,
    s_ref, dk_acc, dv_acc, out_s, grad_s, *, pieces, piece,
):
    blocks = pieces * piece // TILE
    scale = HD**-0.5
    dot = partial(jnp.dot, preferred_element_type=wide)

    def rows_of(b):
        return pl.ds(pl.multiple_of(b * TILE, TILE), TILE)

    def fold(t, how):
        return how(t.reshape(TILE // 8, 8, TILE), axis=0)

    def gather(r, _):
        src = pl.multiple_of(order_ref[r] * piece, piece)
        dst = pl.multiple_of(r * piece, piece)
        sorted_qkv[pl.ds(dst, piece), :] = qkv_ref[pl.ds(src, piece), :]
        sorted_do[pl.ds(dst, piece), :] = do_ref[pl.ds(src, piece), :]
        return 0

    lax.fori_loop(0, pieces, gather, 0)
    first = lax.broadcasted_iota(jnp.int32, (TILE, PAIR), 1) < HD

    def turn(t, rows, sign):
        up = pltpu.roll(t, PAIR - ROT // 2, 1) * up_ref[rows, :]
        down = pltpu.roll(t, ROT // 2, 1) * down_ref[rows, :]
        return t * cos_ref[rows, :] + sign * (up + down)

    def prepare(b, _):
        rows = rows_of(b)
        q = turn(sorted_qkv[rows, 0:PAIR], rows, 1.0).astype(low).astype(wide) * scale
        k = turn(sorted_qkv[rows, PAIR : 2 * PAIR], rows, 1.0)
        v = sorted_qkv[rows, 2 * PAIR : 3 * PAIR]
        g = sorted_do[rows, :].astype(wide)
        for val, nat, tr in ((q, q_nat, q_t), (k, k_nat, k_t), (v, v_nat, v_t), (g, do_nat, do_t)):
            nat[0, b] = jnp.where(first, val, 0.0).astype(low)
            nat[1, b] = jnp.where(first, 0.0, val).astype(low)
            tr[b] = val.T.astype(low)
        dk_acc[b] = jnp.zeros((TILE, PAIR), wide)
        dv_acc[b] = jnp.zeros((TILE, PAIR), wide)
        return 0

    for b in range(blocks):
        prepare(b, 0)
    key_row = lax.broadcasted_iota(jnp.int32, (TILE, TILE), 0)
    query_col = lax.broadcasted_iota(jnp.int32, (TILE, TILE), 1)
    allowed = key_row <= query_col

    def one_block(i, _):
        q_i = q_t[i]
        do_i = do_t[i]

        def score(j, tops):
            new = []
            for h in range(2):
                s = dot(k_nat[h, j], q_i)
                s_ref[h, j] = s
                new.append(jnp.maximum(tops[h], fold(s, jnp.max)))
            return tuple(new)

        partial_tops = (jnp.full((8, TILE), masked_fill, wide),) * 2
        for j in range(i):
            partial_tops = score(j, partial_tops)
        tops = []
        for h in range(2):
            s = jnp.where(allowed, dot(k_nat[h, i], q_i), masked_fill)
            s_ref[h, i] = s
            tops.append(
                jnp.max(jnp.maximum(partial_tops[h], fold(s, jnp.max)), axis=0, keepdims=True)
            )

        def weigh(j, carry):
            sums, accs = carry
            new_sums, new_accs = [], []
            for h in range(2):
                p = jnp.exp(s_ref[h, j] - tops[h])
                s_ref[h, j] = p
                new_sums.append(sums[h] + fold(p, jnp.sum))
                new_accs.append(accs[h] + dot(v_t[j, h * HD : (h + 1) * HD, :], p.astype(low)))
            return tuple(new_sums), tuple(new_accs)

        carry = ((jnp.zeros((8, TILE), wide),) * 2, (jnp.zeros((HD, TILE), wide),) * 2)
        for j in range(i + 1):
            carry = weigh(j, carry)
        sums, accs = carry
        invs, deltas, outs = [], [], []
        for h in range(2):
            inv = 1.0 / jnp.sum(sums[h], axis=0, keepdims=True)
            o = accs[h] * inv
            outs.append(o)
            invs.append(inv)
            g = do_i[h * HD : (h + 1) * HD, :].astype(wide)
            deltas.append(jnp.sum(o * g, axis=0, keepdims=True))
        out_s[i] = jnp.concatenate(outs, axis=0).T.astype(low)

        def pull(j, dq):
            new = []
            dv = dk = None
            for h in range(2):
                dp = dot(v_nat[h, j], do_i)
                p = s_ref[h, j] * invs[h]
                ds = (p * (dp - deltas[h])).astype(low)
                dv_h = dot(p.astype(low), do_nat[h, i])
                dk_h = dot(ds, q_nat[h, i])
                dv = dv_h if dv is None else dv + dv_h
                dk = dk_h if dk is None else dk + dk_h
                new.append(dq[h] + dot(k_t[j, h * HD : (h + 1) * HD, :], ds))
            dv_acc[j] += dv
            dk_acc[j] += dk
            return tuple(new)

        dq = (jnp.zeros((HD, TILE), wide),) * 2
        for j in range(i + 1):
            dq = pull(j, dq)
        rows = rows_of(i)
        dq_rows = jnp.concatenate(dq, axis=0).T * scale
        grad_s[rows, 0:PAIR] = turn(dq_rows, rows, -1.0).astype(low)
        return 0

    for b in range(blocks):
        one_block(b, 0)

    def finish(b, _):
        rows = rows_of(b)
        grad_s[rows, PAIR : 2 * PAIR] = turn(dk_acc[b], rows, -1.0).astype(low)
        grad_s[rows, 2 * PAIR : 3 * PAIR] = dv_acc[b].astype(low)
        sorted_do[rows, :] = out_s[b]
        return 0

    for b in range(blocks):
        finish(b, 0)

    def scatter(r, _):
        src = pl.multiple_of(order_ref[r] * piece, piece)
        dst = pl.multiple_of(r * piece, piece)
        mixed_ref[pl.ds(src, piece), :] = sorted_do[pl.ds(dst, piece), :]
        grad_ref[pl.ds(src, piece), :] = grad_s[pl.ds(dst, piece), :]
        return 0

    lax.fori_loop(0, pieces, scatter, 0)


def attention(order, qkv, grad_mixed, tables, deps):
    seq, width = grad_mixed.shape
    pairs = width // PAIR
    pieces = order.shape[0]
    blocks = seq // TILE
    vmem = pltpu.VMEM
    table = pl.BlockSpec((seq, PAIR), lambda p, o: (0, 0))
    one = pl.BlockSpec((seq, PAIR), lambda p, o: (0, p))
    three = pl.BlockSpec((seq, 3 * PAIR), lambda p, o: (0, p))
    kernel = partial(attention_kernel, pieces=pieces, piece=seq // pieces)
    count = len(deps)

    def inner(order_ref, *refs):
        kernel(order_ref, *refs[count:])

    return pl.pallas_call(
        inner,
        grid_spec=pltpu.PrefetchScalarGridSpec(
            num_scalar_prefetch=1,
            grid=(pairs,),
            in_specs=[pl.BlockSpec(memory_space=pl.ANY)] * count + [three, one, table, table, table],
            out_specs=[one, three],
            scratch_shapes=[
                vmem((seq, 3 * PAIR), wide),
                vmem((seq, PAIR), low),
                *[vmem((2, blocks, TILE, PAIR), low)] * 4,
                *[vmem((blocks, PAIR, TILE), low)] * 4,
                vmem((2, blocks, TILE, TILE), wide),
                vmem((blocks, TILE, PAIR), wide),
                vmem((blocks, TILE, PAIR), wide),
                vmem((blocks, TILE, PAIR), low),
                vmem((seq, 3 * PAIR), low),
            ],
        ),
        out_shape=[
            jax.ShapeDtypeStruct((seq, width), low),
            jax.ShapeDtypeStruct((seq, 3 * width), low),
        ],
        compiler_params=pltpu.CompilerParams(
            vmem_limit_bytes=48 * 1024 * 1024, dimension_semantics=("arbitrary",)
        ),
        cost_estimate=pl.CostEstimate(
            flops=pairs * 24 * seq * seq * PAIR, bytes_accessed=30_000_000, transcendentals=0
        ),
        name="attention",
    )(order, *deps, qkv, grad_mixed, *tables)


def call(body, name, grid, flags, in_specs, args, out_specs, out_shape, flops, moved, deps):
    count = len(deps)

    def inner(flag_ref, *refs):
        body(flag_ref, *refs[count:])

    in_specs = [pl.BlockSpec(memory_space=pl.ANY)] * count + in_specs
    args = [*deps, *args]
    return pl.pallas_call(
        inner,
        grid_spec=pltpu.PrefetchScalarGridSpec(
            num_scalar_prefetch=1, grid=grid, in_specs=in_specs, out_specs=out_specs
        ),
        out_shape=out_shape,
        compiler_params=pltpu.CompilerParams(vmem_limit_bytes=vmem_limit),
        cost_estimate=pl.CostEstimate(flops=flops, bytes_accessed=moved, transcendentals=0),
        name=name,
    )(flags, *args)


def quarter(n):
    return (n % 2) * 2 + n // 2


def product_nn(flags, a, chunks, width, kind, extra, deps):
    rows, model = a.shape
    fourth = model // 4
    step = min(rows, 512)
    count = len(chunks)

    def body(flag_ref, *refs):
        left = [ref[...] for ref in refs[:4]]
        outs = refs[4 + count + (extra is not None) :]
        for n in range(count):
            at = slice(n * width, (n + 1) * width)
            got = None
            for q in range(4):
                w = refs[4 + n][q * fourth : (q + 1) * fourth, :]
                one = jnp.dot(left[q], w, preferred_element_type=wide)
                got = one if got is None else got + one
            if kind == "plain":
                outs[0][:, at] = got.astype(low)
                continue
            more = refs[4 + count][:, at]
            if kind == "bias":
                outs[0][:, at] = got + more
            elif kind == "times":
                outs[0][:, at] = (got * more.astype(wide)).astype(low)
            else:
                v = got + more
                sq = v * v
                up = 0.5 + 0.5 * jnp.tanh(v * (gelu_in + gelu_in * gelu_cubic * sq))
                act = v * up
                outs[0][:, at] = act.astype(low)
                inner = 2.0 * gelu_in + 6.0 * gelu_in * gelu_cubic * sq
                outs[1][:, at] = (up + act * (1.0 - up) * inner).astype(low)

    total = count * width
    own = pl.BlockSpec((step, total), lambda i, f: (i, 0))
    in_specs = [
        pl.BlockSpec((step, fourth), partial(lambda col, i, f: (i, col), quarter(q)))
        for q in range(4)
    ]
    args = [a] * 4
    for weight, col in chunks:
        in_specs.append(pl.BlockSpec((model, width), partial(lambda col, i, f: (0, col), col)))
        args.append(weight)
    if kind == "times":
        extra, col = extra
        in_specs.append(pl.BlockSpec((step, total), lambda i, f: (i, col)))
        args.append(extra)
    elif extra is not None:
        in_specs.append(pl.BlockSpec((1, total), lambda i, f: (0, 0)))
        args.append(extra)
    outs = 2 if kind == "gelu" else 1
    out = call(
        body,
        "rows_" + kind,
        (rows // step,),
        flags,
        in_specs,
        args,
        [own] * outs,
        [jax.ShapeDtypeStruct((rows, total), wide if kind == "bias" else low)] * outs,
        2 * rows * model * total,
        2 * (rows * model + model * total + 2 * rows * total),
        deps,
    )
    return out if outs == 2 else out[0]


def product_tn(flags, outs, side, n_ctx, add, deps):
    rows, model = outs[0][0][0].shape
    half = model // 2
    step = half // 2
    d_own = step // n_ctx
    terms = [term for out in outs for term in out]
    count = len(terms)

    def body(flag_ref, *refs):
        n = 0
        for o, out in enumerate(outs):
            at = 0
            for _, _, _, width in out:
                got = lax.dot_general(
                    refs[n][...],
                    refs[count + n][...],
                    (((0,), (0,)), ((), ())),
                    preferred_element_type=wide,
                ).reshape(n_ctx, d_own, width)
                if add is not None:
                    got += refs[2 * count][:, 0, :, at : at + width].astype(wide)
                refs[-len(outs) + o][:, 0, :, at : at + width] = got.astype(low)
                n += 1
                at += width

    totals = [sum(term[3] for term in out) for out in outs]
    out_specs = [pl.BlockSpec((n_ctx, 1, d_own, t), lambda i, f: (0, i, 0, 0)) for t in totals]
    in_specs = [pl.BlockSpec((rows, step), lambda i, f: (0, 2 * (f[0] ^ side) + i))] * count
    in_specs += [
        pl.BlockSpec((rows, width), partial(lambda col, i, f: (0, col), col))
        for _, _, col, width in terms
    ]
    args = [term[0] for term in terms] + [term[1] for term in terms]
    if add is not None:
        in_specs.append(out_specs[0])
        args.append(add)
    return call(
        body,
        "weight_sums",
        (2,),
        flags,
        in_specs,
        args,
        out_specs,
        [jax.ShapeDtypeStruct((n_ctx, 2, d_own, t), low) for t in totals],
        2 * rows * half * sum(totals),
        2 * (rows * half * count + (rows + half) * sum(totals)),
        deps,
    )


def product_nt(flags, lefts, weights, cols, block, rows, add, split, deps):
    model = weights[0].shape[0]
    step = model // 4
    count = len(lefts)
    ks = [k for _, _, k in lefts]

    def body(flag_ref, *refs):
        got = None
        for a, w in zip(refs[:count], refs[count : 2 * count]):
            one = lax.dot_general(
                a[...], w[...], (((1,), (1,)), ((), ())), preferred_element_type=wide
            )
            got = one if got is None else got + one
        if add is not None:
            got += refs[2 * count][...].astype(wide)
        if split:
            refs[-2][...] = got[: rows // 2]
            refs[-1][...] = got[rows // 2 :].astype(low)
        else:
            refs[-1][...] = got.astype(low)

    in_specs = [
        pl.BlockSpec((rows, k), partial(lambda col, j, f: (block, col), col)) for _, col, k in lefts
    ]
    for (_, _, k), col in zip(lefts, cols):
        in_specs.append(pl.BlockSpec((step, k), partial(lambda col, j, f: (quarter(j), col), col)))
    args = [left for left, _, _ in lefts] + list(weights)
    if add is not None:
        in_specs.append(pl.BlockSpec((rows, step), lambda j, f: (0, j)))
        args.append(add)
    kept = rows // 2 if split else rows
    types = [wide, low] if split else [low]
    out = call(
        body,
        "feature_sums",
        (4,),
        flags,
        in_specs,
        args,
        [pl.BlockSpec((kept, step), lambda j, f: (0, j))] * len(types),
        [jax.ShapeDtypeStruct((kept, model), t) for t in types],
        2 * rows * model * sum(ks),
        2 * (rows + model) * sum(ks) + 4 * rows * model,
        deps,
    )
    return out if split else out[0]


def place_two(flags, mine, mine_y, n_seq, n_slot):
    model = mine.shape[1]
    part = n_slot // 4

    def body(flag_ref, mine_ref, other_ref, out_ref):
        own = pl.program_id(2) == flag_ref[1]

        @pl.when(own)
        def _():
            out_ref[...] = mine_ref[...]

        @pl.when(jnp.logical_not(own))
        def _():
            out_ref[...] = other_ref[...]

    piece = pl.BlockSpec((part, model), lambda i, cc, yy, f: ((cc ^ f[0]) * n_seq + i, 0))
    out = call(
        body,
        "place_two",
        (n_seq, 2, 2),
        flags,
        [piece, piece],
        [mine, mine_y],
        pl.BlockSpec((part, model), lambda i, cc, yy, f: (4 * i + 2 * cc + yy, 0)),
        jax.ShapeDtypeStruct((n_seq * n_slot, model), low),
        0,
        8 * n_seq * n_slot * model,
        [],
    )
    return out.reshape(n_seq, n_slot, model)


def place_rows(flags, mine, mine_y, came, n_seq, n_slot, base):
    model = mine.shape[1]
    part = n_slot // 4
    out_type = low if base is None else wide

    def body(flag_ref, *refs):
        own_core = pl.program_id(1) == flag_ref[0]
        own_mp = pl.program_id(2) == flag_ref[1]

        def put(ref):
            got = ref[...]
            refs[-1][...] = got if base is None else refs[3][...].astype(wide) + got.astype(wide)

        @pl.when(own_core & own_mp)
        def _():
            put(refs[0])

        @pl.when(own_core & jnp.logical_not(own_mp))
        def _():
            put(refs[1])

        @pl.when(jnp.logical_not(own_core))
        def _():
            put(refs[2])

    piece = pl.BlockSpec((part, model), lambda i, cc, yy, f: (n_seq * f[0] + i, 0))
    other = pl.BlockSpec((part, model), lambda i, cc, yy, f: (n_seq * (yy ^ f[1]) + i, 0))
    slot = pl.BlockSpec((part, model), lambda i, cc, yy, f: (4 * i + 2 * cc + yy, 0))
    in_specs = [piece, piece, other]
    args = [mine, mine_y, came]
    if base is not None:
        in_specs.append(slot)
        args.append(base.reshape(n_seq * n_slot, model))
    out = call(
        body,
        "place_rows",
        (n_seq, 2, 2),
        flags,
        in_specs,
        args,
        slot,
        jax.ShapeDtypeStruct((n_seq * n_slot, model), out_type),
        0,
        12 * n_seq * n_slot * model,
        [],
    )
    return out.reshape(n_seq, n_slot, model)


def stack_rows(flags, parts, deps):
    rows, model = parts[0].shape
    step = min(rows, 256)
    steps = rows // step

    def body(flag_ref, *refs):
        for n in range(len(parts)):

            @pl.when(pl.program_id(0) == n)
            def _():
                refs[-1][...] = refs[n][...]

    def at(n, i, j, f):
        return (jnp.where(i < n, 0, jnp.where(i > n, steps - 1, j)), 0)

    return call(
        body,
        "stack_rows",
        (len(parts), steps),
        flags,
        [pl.BlockSpec((step, model), partial(at, n)) for n in range(len(parts))],
        list(parts),
        pl.BlockSpec((step, model), lambda i, j, f: (i * steps + j, 0)),
        jax.ShapeDtypeStruct((len(parts) * rows, model), parts[0].dtype),
        0,
        4 * len(parts) * rows * model,
        deps,
    )


def never(*arrays):
    firsts = [v[(0,) * v.ndim] for v in arrays]
    return sum((v != v).astype(jnp.int32) for v in firsts)


def on_device(
    tokens,
    group_order,
    grad_out,
    norm_gain,
    norm_bias,
    w_qkv,
    b_qkv,
    w_out,
    b_out,
    w_fc1,
    b_fc1,
    w_fc2,
    b_fc2,
):
    n_dp = lax.axis_size("x") * lax.axis_size("core")
    n_ctx, n_mp = lax.axis_size("ctx"), lax.axis_size("mp")
    n_seq, n_slot, model = tokens.shape
    groups = group_order.shape[1]
    assert n_dp == 4 and 2 * n_seq == n_ctx == 4
    z, y = lax.axis_index("ctx"), lax.axis_index("mp")
    x, c = lax.axis_index("x"), lax.axis_index("core")
    dp = 2 * x + c
    half = model // 2
    part = n_slot // (2 * n_mp)
    rows_own = n_ctx * part
    block_len = SEQ_LEN // groups
    d_own = w_qkv.shape[0]
    flag_x = x.astype(jnp.int32).reshape(1)
    flag_cy = jnp.stack([c, y]).astype(jnp.int32)

    def to_core(v):
        return lax.ppermute(v, "core", [(0, 1), (1, 0)])

    def to_x(v):
        return lax.ppermute(v, "x", [(0, 1), (1, 0)])

    def to_z(v, k):
        return lax.ppermute(v, "ctx", [(i, i ^ k) for i in range(n_ctx)])

    def to_y(v):
        return lax.ppermute(v, "mp", [(0, 1), (1, 0)])

    def in_order(bit, mine, other, axis):
        return jnp.where(
            bit == 0,
            jnp.concatenate([mine, other], axis),
            jnp.concatenate([other, mine], axis),
        )

    def to_ctx(v):
        return lax.all_to_all(v, "ctx", 0, 0, tiled=True)

    def send_away(v, wait=0):
        cut = v.reshape(n_seq, 2, n_mp, part, model)

        def of_core(at):
            got = lax.dynamic_slice(
                cut, (0, at, y + wait, 0, 0), (n_seq, 1, 1, part, model)
            )
            return got.reshape(n_seq, part, model)

        return to_ctx(in_order(c, of_core(c), to_core(of_core(1 - c)), 0)).reshape(rows_own, model)

    def send_home(v):
        return to_ctx(v.reshape(n_ctx, part, model))

    def other_mp(got, wait=0):
        return to_y(got + jnp.asarray(wait, got.dtype)) if n_mp == 2 else got

    def with_core(got):
        mine = lax.dynamic_slice_in_dim(got, n_seq * c, n_seq, 0)
        other = to_core(lax.dynamic_slice_in_dim(got, n_seq * (1 - c), n_seq, 0))
        return jnp.concatenate([mine, other], axis=0)

    def placed_rows(homes, homes_y):
        if n_mp == 2:
            flat = [v.reshape(rows_own, model) for v in (homes, homes_y)]
            return place_two(flag_cy, *flat, n_seq, n_slot)
        homes = lax.all_gather(homes.reshape(2, n_seq, part, model), "mp", axis=2, tiled=True)
        homes = jnp.where(c == 0, homes, homes[::-1])
        return jnp.swapaxes(homes, 0, 1).reshape(n_seq, n_slot, model)

    def placed_home(got, got_y, base=None):
        def of_core(at):
            return [lax.dynamic_slice_in_dim(v, n_seq * at, n_seq, 0) for v in (got, got_y)]

        if n_mp == 2:
            came = to_core(jnp.concatenate(of_core(1 - c), axis=0))
            flat = [v.reshape(rows_own, model) for v in (got, got_y, came)]
            return place_rows(flag_cy, *flat, n_seq, n_slot, base)
        mine = lax.all_gather(of_core(c)[0], "mp", axis=1, tiled=True)
        other = to_core(lax.all_gather(of_core(1 - c)[0], "mp", axis=1, tiled=True))
        got = jnp.where(c == 0, jnp.stack([mine, other]), jnp.stack([other, mine]))
        got = jnp.swapaxes(got, 0, 1).reshape(n_seq, n_slot, model)
        return got if base is None else base.astype(wide) + got.astype(wide)

    def gather_rows(parts, deps_own, deps_all):
        if n_mp == 2:
            own = stack_rows(flag_x, [*parts, *[to_y(v) for v in parts]], deps_own)
        else:
            own = lax.all_gather(jnp.concatenate(parts, axis=0), "mp", axis=0, tiled=True)
        return stack_rows(flag_x, [own, to_core(own)], deps_all)

    small = jnp.concatenate(
        [norm_gain, norm_bias, b_out, b_fc2, b_qkv.reshape(-1), b_fc1.reshape(-1)]
    )
    small = jnp.pad(small, (0, -small.shape[0] % 128))[None]
    small = in_order(z % 2, small, to_z(small, 1), 0)
    small = in_order(z // 2, small, to_z(small, 2), 0)
    small = in_order(c, small, to_core(small), 0)
    small = in_order(x, small, to_x(small), 0)

    parts_in = send_away(tokens, never(small))

    pairs = w_qkv.shape[2] // PAIR // 2
    head_chunks = 2 if pairs % 2 == 0 else 1
    chunk_pairs = pairs // head_chunks
    qkv_cols = chunk_pairs * 3 * PAIR
    out_cols = chunk_pairs * PAIR
    hid = w_fc1.shape[1] // 2
    mlp_chunks = 2
    mlp_cols = hid // mlp_chunks
    qkv_split = w_qkv.reshape(d_own, 3, 2, head_chunks, chunk_pairs, PAIR).transpose(2, 3, 0, 4, 1, 5)
    qkv_split = qkv_split.reshape(2, head_chunks, d_own, qkv_cols)
    out_split = w_out.T.reshape(d_own, 2, head_chunks, out_cols).transpose(1, 2, 0, 3)
    heads_split = jnp.concatenate([qkv_split, out_split], axis=-1)
    fc1_split = w_fc1.reshape(d_own, 2, hid).transpose(1, 0, 2)
    fc2_split = w_fc2.T.reshape(d_own, 2, hid).transpose(1, 0, 2)

    def swap_cores(split):
        mine = lax.dynamic_index_in_dim(split, c, 0, keepdims=False)
        return mine, to_core(lax.dynamic_index_in_dim(split, 1 - c, 0, keepdims=False))

    def gather_weight(pair, at, width, wait=0):
        mine, other = (v[:, at : at + width] for v in pair)
        shard = in_order(c + wait, mine[None], other[None], 0)
        got = lax.all_gather(shard, ("x", "ctx"), axis=1, tiled=True)
        return got.reshape(model, width)

    first_cols = qkv_cols + out_cols
    heads_w = [gather_weight(swap_cores(heads_split[:, 0]), 0, first_cols)]
    more_split = jnp.concatenate([*(heads_split[:, n] for n in range(1, head_chunks)), fc1_split, fc2_split], axis=-1)
    more_pair = swap_cores(more_split)
    tokens_there = never(parts_in)
    parts_grad = send_away(grad_out, tokens_there)
    for n in range(1, head_chunks):
        heads_w.append(gather_weight(more_pair, (n - 1) * first_cols, first_cols, tokens_there))
    at = (head_chunks - 1) * first_cols
    fc1_w = gather_weight(more_pair, at, hid, tokens_there)
    fc2_w = gather_weight(more_pair, at + hid, hid, tokens_there)

    n_own = n_dp * n_ctx
    at = 0

    def take(count):
        nonlocal at
        got = small[:, at : at + count]
        at += count
        return got

    gain, shift, out_bias, fc2_bias = (take(d_own).reshape(model).astype(wide) for _ in range(4))
    heads_here, dims_here = b_qkv.shape[1:]
    qkv_bias = take(b_qkv.size).reshape(n_own, 3, heads_here, dims_here)
    qkv_bias = qkv_bias.transpose(1, 2, 0, 3).reshape(3, 2, head_chunks, chunk_pairs, PAIR)
    qkv_bias = lax.dynamic_index_in_dim(qkv_bias, c, 1, keepdims=False)
    qkv_bias = qkv_bias.transpose(1, 2, 0, 3).reshape(head_chunks, 1, qkv_cols).astype(wide)
    fc1_bias = take(b_fc1.size).reshape(n_own, b_fc1.shape[0], b_fc1.shape[1])
    fc1_bias = fc1_bias.transpose(1, 0, 2).reshape(2, 1, hid)
    fc1_bias = lax.dynamic_index_in_dim(fc1_bias, c, 0, keepdims=False).astype(wide)

    order_row = jnp.where(z // 2 == c, group_order, to_core(group_order))
    order_row = lax.dynamic_index_in_dim(order_row, z % 2, 0, keepdims=False)
    ids = jnp.arange(2 * n_mp * n_ctx, dtype=jnp.int32)
    at_core = (ids // (n_mp * n_ctx)) ^ c
    at_mp = (ids // n_ctx) % n_mp
    at_mp = at_mp ^ y if n_mp == 2 else at_mp
    at_ctx = ids % n_ctx
    slot = at_ctx * n_slot + at_core * (n_slot // 2) + at_mp * part
    chosen = (slot // block_len)[:, None] == jnp.arange(groups, dtype=jnp.int32)[None, :]
    block_at = jnp.sum(jnp.where(chosen, order_row[None, :], 0), axis=1)
    position = block_at * block_len + slot % block_len
    order = jnp.sum(jnp.where((position // part)[None, :] == ids[:, None], ids[None, :], 0), axis=1)
    tables = rotary_rows(SEQ_LEN)

    rows_in = parts_in.astype(wide)
    row_mean = jnp.mean(rows_in, axis=-1, keepdims=True)
    centered = rows_in - row_mean
    variance = jnp.mean(centered * centered, axis=-1, keepdims=True)
    inv_std = lax.rsqrt(variance + norm_eps)
    normed = centered * inv_std
    ln_out = gather_rows([(normed * gain + shift).astype(low)], [], [parts_grad])
    last = []

    def step(make, *deps):
        nonlocal last
        got = make([*last, *deps])
        last = [got[0] if isinstance(got, (tuple, list)) else got]
        return got

    def rows_step(a, chunks, width, kind, extra=None, deps=()):
        return step(lambda d: product_nn(flag_x, a, chunks, width, kind, extra, d), *deps)

    def far_sums(out, *deps):
        return out, to_x(step(lambda d: product_tn(flag_x, [out], 1, n_ctx, None, d), *deps)[0])

    def near_sums(far, *deps):
        out, came = far
        total = step(lambda d: product_tn(flag_x, [out], 0, n_ctx, came, d), *deps)[0]
        total = total.reshape(half, total.shape[-1])
        return lax.psum_scatter(total, "ctx", scatter_dimension=0, tiled=True)

    def feature_sums(lefts, weights, cols, *deps):
        rows = lefts[0][0].shape[0] // 2

        def run(block, add, split, more):
            return step(
                lambda d: product_nt(flag_x, lefts, weights, cols, block, rows, add, split, d), *more
            )

        came = to_core(run(1, None, False, deps))

        def two(*more):
            if n_mp == 2:
                mine, other = run(0, came, True, more)
                return mine, to_y(other)
            got = run(0, came, False, more)
            return lax.psum_scatter(got, "mp", scatter_dimension=0, tiled=True).astype(wide), None

        return two

    def joined(mine, came):
        return mine if came is None else mine + came.astype(wide)

    chunk_ids = range(head_chunks)
    both = range(mlp_chunks)
    qkv = [rows_step(ln_out, [(heads_w[0], 0)], qkv_cols, "bias", qkv_bias[0])]
    grad_rows = gather_rows([parts_grad], qkv, [])
    pulled = [rows_step(grad_rows, [(heads_w[0], 3)], out_cols, "plain")]
    for n in range(1, head_chunks):
        qkv.append(rows_step(ln_out, [(heads_w[n], 0)], qkv_cols, "bias", qkv_bias[n]))
        pulled.append(rows_step(grad_rows, [(heads_w[n], 3)], out_cols, "plain"))
    heads, heads_out, far_heads = [], [], []
    for n in chunk_ids:
        heads.append(step(lambda d: attention(order, qkv[n], pulled[n], tables, d)))
        mixed, grad_qkv = heads[n]
        heads_out.append([(ln_out, grad_qkv, 0, qkv_cols), (grad_rows, mixed, 0, out_cols)])
        far_heads.append(far_sums(heads_out[n]))
    act, slope = rows_step(ln_out, [(fc1_w, n) for n in both], mlp_cols, "gelu", fc1_bias)
    fc2_out = [[(grad_rows, act, n, mlp_cols)] for n in both]
    far_2a = far_sums(fc2_out[0], far_heads[0][1])
    attn_two = feature_sums([(h[0], 0, out_cols) for h in heads], heads_w, [3] * head_chunks)
    far_2b = far_sums(fc2_out[1])
    grad_heads = [near_sums(far_heads[0])]
    attn_mine, attn_came = attn_two()
    mlp_two = feature_sums([(act, 0, hid)], [fc2_w], [0], far_heads[-1][1])
    grad_heads += [near_sums(far) for far in far_heads[1:]]
    mlp_mine, mlp_came = mlp_two()
    grad_pre = rows_step(grad_rows, [(fc2_w, n) for n in both], mlp_cols, "times", (slope, 0))
    fc1_out = [[(ln_out, grad_pre, n, mlp_cols)] for n in both]
    far_1a = far_sums(fc1_out[0], far_2a[1])
    grad_2 = [near_sums(far_2a, grad_heads[0])]
    ln_two = feature_sums(
        [(grad_pre, 0, hid)] + [(h[1], 0, qkv_cols) for h in heads],
        [fc1_w, *heads_w],
        [0] * (1 + head_chunks),
        *([] if attn_came is None else [attn_came]),
        far_2b[1],
    )
    attn_out = joined(attn_mine, attn_came) + out_bias
    mlp_out = joined(mlp_mine, mlp_came) + fc2_bias
    block_rows = (rows_in + attn_out + mlp_out).astype(low)
    far_1b = far_sums(fc1_out[1], block_rows)
    block_got = send_home(block_rows)
    grad_2.append(near_sums(far_2b, far_1a[1]))
    ln_mine, ln_came = ln_two(block_got)
    grad_1 = [near_sums(far_1a, grad_heads[-1], far_1b[1])]
    block_homes = with_core(block_got)
    block_y = other_mp(block_homes, 0 if ln_came is None else never(ln_came))
    block_out = placed_rows(block_homes, block_y)
    grad_1.append(near_sums(far_1b, grad_2[0], block_out))

    grad_ln = ln_mine if ln_came is None else ln_mine + ln_came.astype(wide)
    scaled = grad_ln * gain
    back = inv_std * (
        scaled
        - jnp.mean(scaled, axis=-1, keepdims=True)
        - normed * jnp.mean(scaled * normed, axis=-1, keepdims=True)
    )
    back = back.astype(low)
    grad_got = send_home(back)
    grad_tokens = placed_home(grad_got, other_mp(grad_got), grad_out)
    gain_sum = jnp.sum(grad_ln * normed, axis=0)
    shift_sum = jnp.sum(grad_ln, axis=0)

    shared = jnp.concatenate(
        [
            gain_sum,
            shift_sum,
            jnp.sum(parts_grad.astype(wide), axis=0),
            jnp.stack(
                [
                    jnp.sum(rows_in * rows_in),
                    jnp.sum(attn_out * attn_out),
                    jnp.sum(mlp_out * mlp_out),
                ]
            ),
            jnp.zeros((125,), wide),
        ]
    )
    own = jnp.concatenate(
        [jnp.sum(v.astype(wide), axis=0) for v in [*(h[1] for h in heads), grad_pre]]
    )
    n_shared = shared.shape[0]
    sums = jnp.concatenate([shared, own])
    sums = sums + to_x(sums)
    sums = sums + to_z(sums, 1)
    sums = sums + to_z(sums, 2)
    if n_mp == 2:
        shared = sums[:n_shared]
        shared = shared + to_y(shared)
    else:
        shared = lax.psum(sums[:n_shared], "mp")
    sums = jnp.concatenate([shared, sums[n_shared:]])
    came = to_core(sums)
    shared = sums[:n_shared] + came[:n_shared]
    own = in_order(c, sums[None, n_shared:], came[None, n_shared:], 0)
    place = dp * n_ctx + z

    def own_slice(v):
        return lax.dynamic_slice_in_dim(v, place * d_own, d_own, 0)

    grad_gain = own_slice(shared[:model])
    grad_shift = own_slice(shared[model : 2 * model])
    grad_bias_out = own_slice(shared[2 * model : 3 * model])
    cells = n_dp * n_seq * SEQ_LEN * model
    root_means = jnp.sqrt(shared[3 * model : 3 * model + 3] / cells)
    n_heads = head_chunks * qkv_cols
    grad_b_qkv = own[:, :n_heads].reshape(2, pairs, 3, PAIR).transpose(2, 0, 1, 3)
    grad_b_qkv = grad_b_qkv.reshape(3, heads_here, HD)
    grad_b_qkv = lax.dynamic_slice_in_dim(grad_b_qkv, place * dims_here, dims_here, 2)
    grad_b_fc1 = own[:, n_heads:].reshape(b_fc1.shape[0], HD)
    grad_b_fc1 = lax.dynamic_slice_in_dim(grad_b_fc1, place * dims_here, dims_here, 1)

    def by_owner(parts):
        whole = jnp.stack([p.reshape(2, d_own, -1) for p in parts], axis=1)
        mine = lax.dynamic_index_in_dim(whole, c, 0, keepdims=True)
        other = to_core(lax.dynamic_index_in_dim(whole, 1 - c, 0, keepdims=True))
        return in_order(c, mine, other, 0)

    def join(v):
        return v.transpose(2, 0, 1, 3).reshape(d_own, -1).astype(wide)

    grad_h = by_owner(grad_heads)
    grad_w_qkv = grad_h[..., :qkv_cols].reshape(2, head_chunks, d_own, chunk_pairs, 3, PAIR)
    grad_w_qkv = grad_w_qkv.transpose(2, 4, 0, 1, 3, 5).reshape(d_own, 3, -1).astype(wide)
    grad_w_out = join(grad_h[..., qkv_cols:]).T
    return (
        block_out,
        grad_tokens,
        grad_gain,
        grad_shift,
        grad_w_qkv,
        grad_b_qkv,
        grad_w_out,
        grad_bias_out,
        join(by_owner(grad_1)),
        grad_b_fc1,
        join(by_owner(grad_2)).T,
        grad_bias_out,
        root_means,
    )


def solution(mesh):
    n_dp, n_ctx, n_mp = (mesh.shape[name] for name in ("dp", "ctx", "mp"))
    split = jax.sharding.Mesh(
        mesh.devices.reshape(n_dp // 2, 2, n_ctx, n_mp), ("x", "core", "ctx", "mp")
    )
    rows = ("x", "core")
    owners = ("x", "core", "ctx")
    return jax.shard_map(
        on_device,
        mesh=split,
        in_specs=(
            P(rows, "ctx", None),
            P(rows, None),
            P(rows, "ctx", None),
            P(owners),
            P(owners),
            P(owners, None, "mp"),
            P(None, "mp", owners),
            P("mp", owners),
            P(owners),
            P(owners, "mp"),
            P("mp", owners),
            P("mp", owners),
            P(owners),
        ),
        out_specs=(
            P(rows, "ctx", None),
            P(rows, "ctx", None),
            P(owners),
            P(owners),
            P(owners, None, "mp"),
            P(None, "mp", owners),
            P("mp", owners),
            P(owners),
            P(owners, "mp"),
            P("mp", owners),
            P("mp", owners),
            P(owners),
            P(),
        ),
        check_vma=False,
    )
```

```python
from functools import partial

import jax
import jax.numpy as jnp
import numpy as np
from jax import lax
from jax.experimental import pallas as pl
from jax.experimental.pallas import tpu as pltpu
from jax.sharding import PartitionSpec as P

HD = 64
ROT = 32
SEQ_LEN = 2048
PAIR = 2 * HD
TILE = 512

norm_eps = 1e-05
rotary_base = 10000.0
masked_fill = -1e30
low = jnp.bfloat16
wide = jnp.float32
gelu_in = (2.0 / 3.141592653589793) ** 0.5
gelu_cubic = 0.044715
vmem_limit = 48 * 1024 * 1024


def rotary_rows(seq):
    half = ROT // 2
    lane = np.arange(PAIR, dtype=np.int32)[None, :] % HD
    inverse = np.power(np.float32(rotary_base), -(lane % half).astype(np.float32) * np.float32(2.0 / ROT))
    angles = np.arange(seq, dtype=np.float32)[:, None] * inverse
    cosine, sine = np.cos(angles), np.sin(angles)
    return tuple(
        jnp.asarray(v.astype(np.float32))
        for v in (
            np.where(lane < ROT, cosine, 1.0),
            np.where(lane < half, -sine, 0.0),
            np.where((lane >= half) & (lane < ROT), sine, 0.0),
        )
    )


def attention_kernel(
    order_ref, qkv_ref, do_ref, cos_ref, up_ref, down_ref, mixed_ref, grad_ref,
    sorted_qkv, sorted_do, q_nat, k_nat, v_nat, do_nat, q_t, k_t, v_t, do_t,
    s_ref, dk_acc, dv_acc, out_s, grad_s, *, pieces, piece,
):
    blocks = pieces * piece // TILE
    scale = HD**-0.5
    dot = partial(jnp.dot, preferred_element_type=wide)

    def rows_of(b):
        return pl.ds(pl.multiple_of(b * TILE, TILE), TILE)

    def fold(t, how):
        return how(t.reshape(TILE // 8, 8, TILE), axis=0)

    def gather(r, _):
        src = pl.multiple_of(order_ref[r] * piece, piece)
        dst = pl.multiple_of(r * piece, piece)
        sorted_qkv[pl.ds(dst, piece), :] = qkv_ref[pl.ds(src, piece), :]
        sorted_do[pl.ds(dst, piece), :] = do_ref[pl.ds(src, piece), :]
        return 0

    lax.fori_loop(0, pieces, gather, 0)
    first = lax.broadcasted_iota(jnp.int32, (TILE, PAIR), 1) < HD

    def turn(t, rows, sign):
        up = pltpu.roll(t, PAIR - ROT // 2, 1) * up_ref[rows, :]
        down = pltpu.roll(t, ROT // 2, 1) * down_ref[rows, :]
        return t * cos_ref[rows, :] + sign * (up + down)

    def prepare(b, _):
        rows = rows_of(b)
        q = turn(sorted_qkv[rows, 0:PAIR], rows, 1.0).astype(low).astype(wide) * scale
        k = turn(sorted_qkv[rows, PAIR : 2 * PAIR], rows, 1.0)
        v = sorted_qkv[rows, 2 * PAIR : 3 * PAIR]
        g = sorted_do[rows, :].astype(wide)
        for val, nat, tr in ((q, q_nat, q_t), (k, k_nat, k_t), (v, v_nat, v_t), (g, do_nat, do_t)):
            nat[0, b] = jnp.where(first, val, 0.0).astype(low)
            nat[1, b] = jnp.where(first, 0.0, val).astype(low)
            tr[b] = val.T.astype(low)
        dk_acc[b] = jnp.zeros((TILE, PAIR), wide)
        dv_acc[b] = jnp.zeros((TILE, PAIR), wide)
        return 0

    for b in range(blocks):
        prepare(b, 0)
    key_row = lax.broadcasted_iota(jnp.int32, (TILE, TILE), 0)
    query_col = lax.broadcasted_iota(jnp.int32, (TILE, TILE), 1)
    allowed = key_row <= query_col

    def one_block(i, _):
        q_i = q_t[i]
        do_i = do_t[i]

        def score(j, tops):
            new = []
            for h in range(2):
                s = dot(k_nat[h, j], q_i)
                s_ref[h, j] = s
                new.append(jnp.maximum(tops[h], fold(s, jnp.max)))
            return tuple(new)

        partial_tops = (jnp.full((8, TILE), masked_fill, wide),) * 2
        for j in range(i):
            partial_tops = score(j, partial_tops)
        tops = []
        for h in range(2):
            s = jnp.where(allowed, dot(k_nat[h, i], q_i), masked_fill)
            s_ref[h, i] = s
            tops.append(
                jnp.max(jnp.maximum(partial_tops[h], fold(s, jnp.max)), axis=0, keepdims=True)
            )

        def weigh(j, carry):
            sums, accs = carry
            new_sums, new_accs = [], []
            for h in range(2):
                p = jnp.exp(s_ref[h, j] - tops[h])
                s_ref[h, j] = p
                new_sums.append(sums[h] + fold(p, jnp.sum))
                new_accs.append(accs[h] + dot(v_t[j, h * HD : (h + 1) * HD, :], p.astype(low)))
            return tuple(new_sums), tuple(new_accs)

        carry = ((jnp.zeros((8, TILE), wide),) * 2, (jnp.zeros((HD, TILE), wide),) * 2)
        for j in range(i + 1):
            carry = weigh(j, carry)
        sums, accs = carry
        invs, deltas, outs = [], [], []
        for h in range(2):
            inv = 1.0 / jnp.sum(sums[h], axis=0, keepdims=True)
            o = accs[h] * inv
            outs.append(o)
            invs.append(inv)
            g = do_i[h * HD : (h + 1) * HD, :].astype(wide)
            deltas.append(jnp.sum(o * g, axis=0, keepdims=True))
        out_s[i] = jnp.concatenate(outs, axis=0).T.astype(low)

        def pull(j, dq):
            new = []
            dv = dk = None
            for h in range(2):
                dp = dot(v_nat[h, j], do_i)
                p = s_ref[h, j] * invs[h]
                ds = (p * (dp - deltas[h])).astype(low)
                dv_h = dot(p.astype(low), do_nat[h, i])
                dk_h = dot(ds, q_nat[h, i])
                dv = dv_h if dv is None else dv + dv_h
                dk = dk_h if dk is None else dk + dk_h
                new.append(dq[h] + dot(k_t[j, h * HD : (h + 1) * HD, :], ds))
            dv_acc[j] += dv
            dk_acc[j] += dk
            return tuple(new)

        dq = (jnp.zeros((HD, TILE), wide),) * 2
        for j in range(i + 1):
            dq = pull(j, dq)
        rows = rows_of(i)
        dq_rows = jnp.concatenate(dq, axis=0).T * scale
        grad_s[rows, 0:PAIR] = turn(dq_rows, rows, -1.0).astype(low)
        return 0

    for b in range(blocks):
        one_block(b, 0)

    def finish(b, _):
        rows = rows_of(b)
        grad_s[rows, PAIR : 2 * PAIR] = turn(dk_acc[b], rows, -1.0).astype(low)
        grad_s[rows, 2 * PAIR : 3 * PAIR] = dv_acc[b].astype(low)
        sorted_do[rows, :] = out_s[b]
        return 0

    for b in range(blocks):
        finish(b, 0)

    def scatter(r, _):
        src = pl.multiple_of(order_ref[r] * piece, piece)
        dst = pl.multiple_of(r * piece, piece)
        mixed_ref[pl.ds(src, piece), :] = sorted_do[pl.ds(dst, piece), :]
        grad_ref[pl.ds(src, piece), :] = grad_s[pl.ds(dst, piece), :]
        return 0

    lax.fori_loop(0, pieces, scatter, 0)


def attention(order, qkv, grad_mixed, tables, deps):
    seq, width = grad_mixed.shape
    pairs = width // PAIR
    pieces = order.shape[0]
    blocks = seq // TILE
    vmem = pltpu.VMEM
    table = pl.BlockSpec((seq, PAIR), lambda p, o: (0, 0))
    one = pl.BlockSpec((seq, PAIR), lambda p, o: (0, p))
    three = pl.BlockSpec((seq, 3 * PAIR), lambda p, o: (0, p))
    kernel = partial(attention_kernel, pieces=pieces, piece=seq // pieces)
    count = len(deps)

    def inner(order_ref, *refs):
        kernel(order_ref, *refs[count:])

    return pl.pallas_call(
        inner,
        grid_spec=pltpu.PrefetchScalarGridSpec(
            num_scalar_prefetch=1,
            grid=(pairs,),
            in_specs=[pl.BlockSpec(memory_space=pl.ANY)] * count + [three, one, table, table, table],
            out_specs=[one, three],
            scratch_shapes=[
                vmem((seq, 3 * PAIR), wide),
                vmem((seq, PAIR), low),
                *[vmem((2, blocks, TILE, PAIR), low)] * 4,
                *[vmem((blocks, PAIR, TILE), low)] * 4,
                vmem((2, blocks, TILE, TILE), wide),
                vmem((blocks, TILE, PAIR), wide),
                vmem((blocks, TILE, PAIR), wide),
                vmem((blocks, TILE, PAIR), low),
                vmem((seq, 3 * PAIR), low),
            ],
        ),
        out_shape=[
            jax.ShapeDtypeStruct((seq, width), low),
            jax.ShapeDtypeStruct((seq, 3 * width), low),
        ],
        compiler_params=pltpu.CompilerParams(
            vmem_limit_bytes=48 * 1024 * 1024, dimension_semantics=("arbitrary",)
        ),
        cost_estimate=pl.CostEstimate(
            flops=pairs * 24 * seq * seq * PAIR, bytes_accessed=30_000_000, transcendentals=0
        ),
        name="attention",
    )(order, *deps, qkv, grad_mixed, *tables)


def call(body, name, grid, flags, in_specs, args, out_specs, out_shape, flops, moved, deps):
    count = len(deps)

    def inner(flag_ref, *refs):
        body(flag_ref, *refs[count:])

    in_specs = [pl.BlockSpec(memory_space=pl.ANY)] * count + in_specs
    args = [*deps, *args]
    return pl.pallas_call(
        inner,
        grid_spec=pltpu.PrefetchScalarGridSpec(
            num_scalar_prefetch=1, grid=grid, in_specs=in_specs, out_specs=out_specs
        ),
        out_shape=out_shape,
        compiler_params=pltpu.CompilerParams(vmem_limit_bytes=vmem_limit),
        cost_estimate=pl.CostEstimate(flops=flops, bytes_accessed=moved, transcendentals=0),
        name=name,
    )(flags, *args)


def quarter(n):
    return (n % 2) * 2 + n // 2


def product_nn(flags, a, chunks, width, kind, extra, deps):
    rows, model = a.shape
    fourth = model // 4
    step = min(rows, 512)
    count = len(chunks)

    def body(flag_ref, *refs):
        left = [ref[...] for ref in refs[:4]]
        outs = refs[4 + count + (extra is not None) :]
        for n in range(count):
            at = slice(n * width, (n + 1) * width)
            got = None
            for q in range(4):
                w = refs[4 + n][q * fourth : (q + 1) * fourth, :]
                one = jnp.dot(left[q], w, preferred_element_type=wide)
                got = one if got is None else got + one
            if kind == "plain":
                outs[0][:, at] = got.astype(low)
                continue
            more = refs[4 + count][:, at]
            if kind == "bias":
                outs[0][:, at] = got + more
            elif kind == "times":
                outs[0][:, at] = (got * more.astype(wide)).astype(low)
            else:
                v = got + more
                sq = v * v
                up = 0.5 + 0.5 * jnp.tanh(v * (gelu_in + gelu_in * gelu_cubic * sq))
                act = v * up
                outs[0][:, at] = act.astype(low)
                inner = 2.0 * gelu_in + 6.0 * gelu_in * gelu_cubic * sq
                outs[1][:, at] = (up + act * (1.0 - up) * inner).astype(low)

    total = count * width
    own = pl.BlockSpec((step, total), lambda i, f: (i, 0))
    in_specs = [
        pl.BlockSpec((step, fourth), partial(lambda col, i, f: (i, col), quarter(q)))
        for q in range(4)
    ]
    args = [a] * 4
    for weight, col in chunks:
        in_specs.append(pl.BlockSpec((model, width), partial(lambda col, i, f: (0, col), col)))
        args.append(weight)
    if kind == "times":
        extra, col = extra
        in_specs.append(pl.BlockSpec((step, total), lambda i, f: (i, col)))
        args.append(extra)
    elif extra is not None:
        in_specs.append(pl.BlockSpec((1, total), lambda i, f: (0, 0)))
        args.append(extra)
    outs = 2 if kind == "gelu" else 1
    out = call(
        body,
        "rows_" + kind,
        (rows // step,),
        flags,
        in_specs,
        args,
        [own] * outs,
        [jax.ShapeDtypeStruct((rows, total), wide if kind == "bias" else low)] * outs,
        2 * rows * model * total,
        2 * (rows * model + model * total + 2 * rows * total),
        deps,
    )
    return out if outs == 2 else out[0]


def product_tn(flags, outs, side, n_ctx, add, deps):
    rows, model = outs[0][0][0].shape
    half = model // 2
    step = half // 2
    d_own = step // n_ctx
    terms = [term for out in outs for term in out]
    count = len(terms)

    def body(flag_ref, *refs):
        n = 0
        for o, out in enumerate(outs):
            at = 0
            for _, _, _, width in out:
                got = lax.dot_general(
                    refs[n][...],
                    refs[count + n][...],
                    (((0,), (0,)), ((), ())),
                    preferred_element_type=wide,
                ).reshape(n_ctx, d_own, width)
                if add is not None:
                    got += refs[2 * count][:, 0, :, at : at + width].astype(wide)
                refs[-len(outs) + o][:, 0, :, at : at + width] = got.astype(low)
                n += 1
                at += width

    totals = [sum(term[3] for term in out) for out in outs]
    out_specs = [pl.BlockSpec((n_ctx, 1, d_own, t), lambda i, f: (0, i, 0, 0)) for t in totals]
    in_specs = [pl.BlockSpec((rows, step), lambda i, f: (0, 2 * (f[0] ^ side) + i))] * count
    in_specs += [
        pl.BlockSpec((rows, width), partial(lambda col, i, f: (0, col), col))
        for _, _, col, width in terms
    ]
    args = [term[0] for term in terms] + [term[1] for term in terms]
    if add is not None:
        in_specs.append(out_specs[0])
        args.append(add)
    return call(
        body,
        "weight_sums",
        (2,),
        flags,
        in_specs,
        args,
        out_specs,
        [jax.ShapeDtypeStruct((n_ctx, 2, d_own, t), low) for t in totals],
        2 * rows * half * sum(totals),
        2 * (rows * half * count + (rows + half) * sum(totals)),
        deps,
    )


def product_nt(flags, lefts, weights, cols, block, rows, add, split, deps):
    model = weights[0].shape[0]
    step = model // 4
    count = len(lefts)
    ks = [k for _, _, k in lefts]

    def body(flag_ref, *refs):
        got = None
        for a, w in zip(refs[:count], refs[count : 2 * count]):
            one = lax.dot_general(
                a[...], w[...], (((1,), (1,)), ((), ())), preferred_element_type=wide
            )
            got = one if got is None else got + one
        if add is not None:
            got += refs[2 * count][...].astype(wide)
        if split:
            refs[-2][...] = got[: rows // 2]
            refs[-1][...] = got[rows // 2 :].astype(low)
        else:
            refs[-1][...] = got.astype(low)

    in_specs = [
        pl.BlockSpec((rows, k), partial(lambda col, j, f: (block, col), col)) for _, col, k in lefts
    ]
    for (_, _, k), col in zip(lefts, cols):
        in_specs.append(pl.BlockSpec((step, k), partial(lambda col, j, f: (quarter(j), col), col)))
    args = [left for left, _, _ in lefts] + list(weights)
    if add is not None:
        in_specs.append(pl.BlockSpec((rows, step), lambda j, f: (0, j)))
        args.append(add)
    kept = rows // 2 if split else rows
    types = [wide, low] if split else [low]
    out = call(
        body,
        "feature_sums",
        (4,),
        flags,
        in_specs,
        args,
        [pl.BlockSpec((kept, step), lambda j, f: (0, j))] * len(types),
        [jax.ShapeDtypeStruct((kept, model), t) for t in types],
        2 * rows * model * sum(ks),
        2 * (rows + model) * sum(ks) + 4 * rows * model,
        deps,
    )
    return out if split else out[0]


def place_two(flags, mine, mine_y, n_seq, n_slot):
    model = mine.shape[1]
    part = n_slot // 4

    def body(flag_ref, mine_ref, other_ref, out_ref):
        own = pl.program_id(2) == flag_ref[1]

        @pl.when(own)
        def _():
            out_ref[...] = mine_ref[...]

        @pl.when(jnp.logical_not(own))
        def _():
            out_ref[...] = other_ref[...]

    piece = pl.BlockSpec((part, model), lambda i, cc, yy, f: ((cc ^ f[0]) * n_seq + i, 0))
    out = call(
        body,
        "place_two",
        (n_seq, 2, 2),
        flags,
        [piece, piece],
        [mine, mine_y],
        pl.BlockSpec((part, model), lambda i, cc, yy, f: (4 * i + 2 * cc + yy, 0)),
        jax.ShapeDtypeStruct((n_seq * n_slot, model), low),
        0,
        8 * n_seq * n_slot * model,
        [],
    )
    return out.reshape(n_seq, n_slot, model)


def place_rows(flags, mine, mine_y, came, n_seq, n_slot, base):
    model = mine.shape[1]
    part = n_slot // 4
    out_type = low if base is None else wide

    def body(flag_ref, *refs):
        own_core = pl.program_id(1) == flag_ref[0]
        own_mp = pl.program_id(2) == flag_ref[1]

        def put(ref):
            got = ref[...]
            refs[-1][...] = got if base is None else refs[3][...].astype(wide) + got.astype(wide)

        @pl.when(own_core & own_mp)
        def _():
            put(refs[0])

        @pl.when(own_core & jnp.logical_not(own_mp))
        def _():
            put(refs[1])

        @pl.when(jnp.logical_not(own_core))
        def _():
            put(refs[2])

    piece = pl.BlockSpec((part, model), lambda i, cc, yy, f: (n_seq * f[0] + i, 0))
    other = pl.BlockSpec((part, model), lambda i, cc, yy, f: (n_seq * (yy ^ f[1]) + i, 0))
    slot = pl.BlockSpec((part, model), lambda i, cc, yy, f: (4 * i + 2 * cc + yy, 0))
    in_specs = [piece, piece, other]
    args = [mine, mine_y, came]
    if base is not None:
        in_specs.append(slot)
        args.append(base.reshape(n_seq * n_slot, model))
    out = call(
        body,
        "place_rows",
        (n_seq, 2, 2),
        flags,
        in_specs,
        args,
        slot,
        jax.ShapeDtypeStruct((n_seq * n_slot, model), out_type),
        0,
        12 * n_seq * n_slot * model,
        [],
    )
    return out.reshape(n_seq, n_slot, model)


def stack_rows(flags, parts, deps):
    rows, model = parts[0].shape
    step = min(rows, 256)
    steps = rows // step

    def body(flag_ref, *refs):
        for n in range(len(parts)):

            @pl.when(pl.program_id(0) == n)
            def _():
                refs[-1][...] = refs[n][...]

    def at(n, i, j, f):
        return (jnp.where(i < n, 0, jnp.where(i > n, steps - 1, j)), 0)

    return call(
        body,
        "stack_rows",
        (len(parts), steps),
        flags,
        [pl.BlockSpec((step, model), partial(at, n)) for n in range(len(parts))],
        list(parts),
        pl.BlockSpec((step, model), lambda i, j, f: (i * steps + j, 0)),
        jax.ShapeDtypeStruct((len(parts) * rows, model), parts[0].dtype),
        0,
        4 * len(parts) * rows * model,
        deps,
    )


def never(*arrays):
    firsts = [v[(0,) * v.ndim] for v in arrays]
    return sum((v != v).astype(jnp.int32) for v in firsts)


def on_device(
    tokens,
    group_order,
    grad_out,
    norm_gain,
    norm_bias,
    w_qkv,
    b_qkv,
    w_out,
    b_out,
    w_fc1,
    b_fc1,
    w_fc2,
    b_fc2,
):
    n_dp = lax.axis_size("x") * lax.axis_size("core")
    n_ctx, n_mp = lax.axis_size("ctx"), lax.axis_size("mp")
    n_seq, n_slot, model = tokens.shape
    groups = group_order.shape[1]
    assert n_dp == 4 and 2 * n_seq == n_ctx == 4
    z, y = lax.axis_index("ctx"), lax.axis_index("mp")
    x, c = lax.axis_index("x"), lax.axis_index("core")
    dp = 2 * x + c
    half = model // 2
    part = n_slot // (2 * n_mp)
    rows_own = n_ctx * part
    block_len = SEQ_LEN // groups
    d_own = w_qkv.shape[0]
    flag_x = x.astype(jnp.int32).reshape(1)
    flag_cy = jnp.stack([c, y]).astype(jnp.int32)

    def to_core(v):
        return lax.ppermute(v, "core", [(0, 1), (1, 0)])

    def to_x(v):
        return lax.ppermute(v, "x", [(0, 1), (1, 0)])

    def to_z(v, k):
        return lax.ppermute(v, "ctx", [(i, i ^ k) for i in range(n_ctx)])

    def to_y(v):
        return lax.ppermute(v, "mp", [(0, 1), (1, 0)])

    def in_order(bit, mine, other, axis):
        return jnp.where(
            bit == 0,
            jnp.concatenate([mine, other], axis),
            jnp.concatenate([other, mine], axis),
        )

    def to_ctx(v):
        return lax.all_to_all(v, "ctx", 0, 0, tiled=True)

    def send_away(v, wait=0):
        cut = v.reshape(n_seq, 2, n_mp, part, model)

        def of_core(at):
            got = lax.dynamic_slice(
                cut, (0, at, y + wait, 0, 0), (n_seq, 1, 1, part, model)
            )
            return got.reshape(n_seq, part, model)

        return to_ctx(in_order(c, of_core(c), to_core(of_core(1 - c)), 0)).reshape(rows_own, model)

    def send_home(v):
        return to_ctx(v.reshape(n_ctx, part, model))

    def other_mp(got, wait=0):
        return to_y(got + jnp.asarray(wait, got.dtype)) if n_mp == 2 else got

    def with_core(got):
        mine = lax.dynamic_slice_in_dim(got, n_seq * c, n_seq, 0)
        other = to_core(lax.dynamic_slice_in_dim(got, n_seq * (1 - c), n_seq, 0))
        return jnp.concatenate([mine, other], axis=0)

    def placed_rows(homes, homes_y):
        if n_mp == 2:
            flat = [v.reshape(rows_own, model) for v in (homes, homes_y)]
            return place_two(flag_cy, *flat, n_seq, n_slot)
        homes = lax.all_gather(homes.reshape(2, n_seq, part, model), "mp", axis=2, tiled=True)
        homes = jnp.where(c == 0, homes, homes[::-1])
        return jnp.swapaxes(homes, 0, 1).reshape(n_seq, n_slot, model)

    def placed_home(got, got_y, base=None):
        def of_core(at):
            return [lax.dynamic_slice_in_dim(v, n_seq * at, n_seq, 0) for v in (got, got_y)]

        if n_mp == 2:
            came = to_core(jnp.concatenate(of_core(1 - c), axis=0))
            flat = [v.reshape(rows_own, model) for v in (got, got_y, came)]
            return place_rows(flag_cy, *flat, n_seq, n_slot, base)
        mine = lax.all_gather(of_core(c)[0], "mp", axis=1, tiled=True)
        other = to_core(lax.all_gather(of_core(1 - c)[0], "mp", axis=1, tiled=True))
        got = jnp.where(c == 0, jnp.stack([mine, other]), jnp.stack([other, mine]))
        got = jnp.swapaxes(got, 0, 1).reshape(n_seq, n_slot, model)
        return got if base is None else base.astype(wide) + got.astype(wide)

    def gather_rows(parts, deps_own, deps_all):
        if n_mp == 2:
            own = stack_rows(flag_x, [*parts, *[to_y(v) for v in parts]], deps_own)
        else:
            own = lax.all_gather(jnp.concatenate(parts, axis=0), "mp", axis=0, tiled=True)
        return stack_rows(flag_x, [own, to_core(own)], deps_all)

    small = jnp.concatenate(
        [norm_gain, norm_bias, b_out, b_fc2, b_qkv.reshape(-1), b_fc1.reshape(-1)]
    )
    small = jnp.pad(small, (0, -small.shape[0] % 128))[None]
    small = in_order(z % 2, small, to_z(small, 1), 0)
    small = in_order(z // 2, small, to_z(small, 2), 0)
    small = in_order(c, small, to_core(small), 0)
    small = in_order(x, small, to_x(small), 0)

    parts_in = send_away(tokens, never(small))

    pairs = w_qkv.shape[2] // PAIR // 2
    head_chunks = 2 if pairs % 2 == 0 else 1
    chunk_pairs = pairs // head_chunks
    qkv_cols = chunk_pairs * 3 * PAIR
    out_cols = chunk_pairs * PAIR
    hid = w_fc1.shape[1] // 2
    mlp_chunks = 2
    mlp_cols = hid // mlp_chunks
    qkv_split = w_qkv.reshape(d_own, 3, 2, head_chunks, chunk_pairs, PAIR).transpose(2, 3, 0, 4, 1, 5)
    qkv_split = qkv_split.reshape(2, head_chunks, d_own, qkv_cols)
    out_split = w_out.T.reshape(d_own, 2, head_chunks, out_cols).transpose(1, 2, 0, 3)
    heads_split = jnp.concatenate([qkv_split, out_split], axis=-1)
    fc1_split = w_fc1.reshape(d_own, 2, hid).transpose(1, 0, 2)
    fc2_split = w_fc2.T.reshape(d_own, 2, hid).transpose(1, 0, 2)

    def swap_cores(split):
        mine = lax.dynamic_index_in_dim(split, c, 0, keepdims=False)
        return mine, to_core(lax.dynamic_index_in_dim(split, 1 - c, 0, keepdims=False))

    def gather_weight(pair, at, width, wait=0):
        mine, other = (v[:, at : at + width] for v in pair)
        shard = in_order(c + wait, mine[None], other[None], 0)
        got = lax.all_gather(shard, ("x", "ctx"), axis=1, tiled=True)
        return got.reshape(model, width)

    first_cols = qkv_cols + out_cols
    heads_w = [gather_weight(swap_cores(heads_split[:, 0]), 0, first_cols)]
    more_split = jnp.concatenate([*(heads_split[:, n] for n in range(1, head_chunks)), fc1_split, fc2_split], axis=-1)
    more_pair = swap_cores(more_split)
    tokens_there = never(parts_in)
    parts_grad = send_away(grad_out, tokens_there)
    for n in range(1, head_chunks):
        heads_w.append(gather_weight(more_pair, (n - 1) * first_cols, first_cols, tokens_there))
    at = (head_chunks - 1) * first_cols
    fc1_w = gather_weight(more_pair, at, hid, tokens_there)
    fc2_w = gather_weight(more_pair, at + hid, hid, tokens_there)

    n_own = n_dp * n_ctx
    at = 0

    def take(count):
        nonlocal at
        got = small[:, at : at + count]
        at += count
        return got

    gain, shift, out_bias, fc2_bias = (take(d_own).reshape(model).astype(wide) for _ in range(4))
    heads_here, dims_here = b_qkv.shape[1:]
    qkv_bias = take(b_qkv.size).reshape(n_own, 3, heads_here, dims_here)
    qkv_bias = qkv_bias.transpose(1, 2, 0, 3).reshape(3, 2, head_chunks, chunk_pairs, PAIR)
    qkv_bias = lax.dynamic_index_in_dim(qkv_bias, c, 1, keepdims=False)
    qkv_bias = qkv_bias.transpose(1, 2, 0, 3).reshape(head_chunks, 1, qkv_cols).astype(wide)
    fc1_bias = take(b_fc1.size).reshape(n_own, b_fc1.shape[0], b_fc1.shape[1])
    fc1_bias = fc1_bias.transpose(1, 0, 2).reshape(2, 1, hid)
    fc1_bias = lax.dynamic_index_in_dim(fc1_bias, c, 0, keepdims=False).astype(wide)

    order_row = jnp.where(z // 2 == c, group_order, to_core(group_order))
    order_row = lax.dynamic_index_in_dim(order_row, z % 2, 0, keepdims=False)
    ids = jnp.arange(2 * n_mp * n_ctx, dtype=jnp.int32)
    at_core = (ids // (n_mp * n_ctx)) ^ c
    at_mp = (ids // n_ctx) % n_mp
    at_mp = at_mp ^ y if n_mp == 2 else at_mp
    at_ctx = ids % n_ctx
    slot = at_ctx * n_slot + at_core * (n_slot // 2) + at_mp * part
    chosen = (slot // block_len)[:, None] == jnp.arange(groups, dtype=jnp.int32)[None, :]
    block_at = jnp.sum(jnp.where(chosen, order_row[None, :], 0), axis=1)
    position = block_at * block_len + slot % block_len
    order = jnp.sum(jnp.where((position // part)[None, :] == ids[:, None], ids[None, :], 0), axis=1)
    tables = rotary_rows(SEQ_LEN)

    rows_in = parts_in.astype(wide)
    row_mean = jnp.mean(rows_in, axis=-1, keepdims=True)
    centered = rows_in - row_mean
    variance = jnp.mean(centered * centered, axis=-1, keepdims=True)
    inv_std = lax.rsqrt(variance + norm_eps)
    normed = centered * inv_std
    ln_out = gather_rows([(normed * gain + shift).astype(low)], [], [parts_grad])
    last = []

    def step(make, *deps):
        nonlocal last
        got = make([*last, *deps])
        last = [got[0] if isinstance(got, (tuple, list)) else got]
        return got

    def rows_step(a, chunks, width, kind, extra=None, deps=()):
        return step(lambda d: product_nn(flag_x, a, chunks, width, kind, extra, d), *deps)

    def far_sums(out, *deps):
        return out, to_x(step(lambda d: product_tn(flag_x, [out], 1, n_ctx, None, d), *deps)[0])

    def near_sums(far, *deps):
        out, came = far
        total = step(lambda d: product_tn(flag_x, [out], 0, n_ctx, came, d), *deps)[0]
        total = total.reshape(half, total.shape[-1])
        return lax.psum_scatter(total, "ctx", scatter_dimension=0, tiled=True)

    def feature_sums(lefts, weights, cols, *deps):
        rows = lefts[0][0].shape[0] // 2

        def run(block, add, split, more):
            return step(
                lambda d: product_nt(flag_x, lefts, weights, cols, block, rows, add, split, d), *more
            )

        came = to_core(run(1, None, False, deps))

        def two(*more):
            if n_mp == 2:
                mine, other = run(0, came, True, more)
                return mine, to_y(other)
            got = run(0, came, False, more)
            return lax.psum_scatter(got, "mp", scatter_dimension=0, tiled=True).astype(wide), None

        return two

    def joined(mine, came):
        return mine if came is None else mine + came.astype(wide)

    chunk_ids = range(head_chunks)
    both = range(mlp_chunks)
    qkv = [rows_step(ln_out, [(heads_w[0], 0)], qkv_cols, "bias", qkv_bias[0])]
    grad_rows = gather_rows([parts_grad], qkv, [])
    pulled = [rows_step(grad_rows, [(heads_w[0], 3)], out_cols, "plain")]
    for n in range(1, head_chunks):
        qkv.append(rows_step(ln_out, [(heads_w[n], 0)], qkv_cols, "bias", qkv_bias[n]))
        pulled.append(rows_step(grad_rows, [(heads_w[n], 3)], out_cols, "plain"))
    heads, heads_out, far_heads = [], [], []
    for n in chunk_ids:
        heads.append(step(lambda d: attention(order, qkv[n], pulled[n], tables, d)))
        mixed, grad_qkv = heads[n]
        heads_out.append([(ln_out, grad_qkv, 0, qkv_cols), (grad_rows, mixed, 0, out_cols)])
        far_heads.append(far_sums(heads_out[n]))
    act, slope = rows_step(ln_out, [(fc1_w, n) for n in both], mlp_cols, "gelu", fc1_bias)
    fc2_out = [[(grad_rows, act, n, mlp_cols)] for n in both]
    far_2a = far_sums(fc2_out[0], far_heads[0][1])
    attn_two = feature_sums([(h[0], 0, out_cols) for h in heads], heads_w, [3] * head_chunks)
    far_2b = far_sums(fc2_out[1])
    grad_heads = [near_sums(far_heads[0])]
    attn_mine, attn_came = attn_two()
    grad_pre = rows_step(grad_rows, [(fc2_w, n) for n in both], mlp_cols, "times", (slope, 0))
    mlp_two = feature_sums([(act, 0, hid)], [fc2_w], [0], far_heads[-1][1])
    grad_heads += [near_sums(far) for far in far_heads[1:]]
    mlp_mine, mlp_came = mlp_two()
    fc1_out = [[(ln_out, grad_pre, n, mlp_cols)] for n in both]
    far_1a = far_sums(fc1_out[0], far_2a[1])
    grad_2 = [near_sums(far_2a, grad_heads[0])]
    ln_two = feature_sums(
        [(grad_pre, 0, hid)] + [(h[1], 0, qkv_cols) for h in heads],
        [fc1_w, *heads_w],
        [0] * (1 + head_chunks),
        *([] if attn_came is None else [attn_came]),
        far_2b[1],
    )
    attn_out = joined(attn_mine, attn_came) + out_bias
    mlp_out = joined(mlp_mine, mlp_came) + fc2_bias
    block_rows = (rows_in + attn_out + mlp_out).astype(low)
    far_1b = far_sums(fc1_out[1], block_rows)
    block_got = send_home(block_rows)
    grad_2.append(near_sums(far_2b, far_1a[1]))
    ln_mine, ln_came = ln_two(block_got)
    grad_1 = [near_sums(far_1a, grad_heads[-1], far_1b[1])]
    block_homes = with_core(block_got)
    block_y = other_mp(block_homes, 0 if ln_came is None else never(ln_came))
    block_out = placed_rows(block_homes, block_y)
    grad_1.append(near_sums(far_1b, grad_2[0], block_out))

    grad_ln = ln_mine if ln_came is None else ln_mine + ln_came.astype(wide)
    scaled = grad_ln * gain
    back = inv_std * (
        scaled
        - jnp.mean(scaled, axis=-1, keepdims=True)
        - normed * jnp.mean(scaled * normed, axis=-1, keepdims=True)
    )
    back = back.astype(low)
    grad_got = send_home(back)
    grad_tokens = placed_home(grad_got, other_mp(grad_got), grad_out)
    gain_sum = jnp.sum(grad_ln * normed, axis=0)
    shift_sum = jnp.sum(grad_ln, axis=0)

    shared = jnp.concatenate(
        [
            gain_sum,
            shift_sum,
            jnp.sum(parts_grad.astype(wide), axis=0),
            jnp.stack(
                [
                    jnp.sum(rows_in * rows_in),
                    jnp.sum(attn_out * attn_out),
                    jnp.sum(mlp_out * mlp_out),
                ]
            ),
            jnp.zeros((125,), wide),
        ]
    )
    own = jnp.concatenate(
        [jnp.sum(v.astype(wide), axis=0) for v in [*(h[1] for h in heads), grad_pre]]
    )
    n_shared = shared.shape[0]
    sums = jnp.concatenate([shared, own])
    sums = sums + to_x(sums)
    sums = sums + to_z(sums, 1)
    sums = sums + to_z(sums, 2)
    if n_mp == 2:
        shared = sums[:n_shared]
        shared = shared + to_y(shared)
    else:
        shared = lax.psum(sums[:n_shared], "mp")
    sums = jnp.concatenate([shared, sums[n_shared:]])
    came = to_core(sums)
    shared = sums[:n_shared] + came[:n_shared]
    own = in_order(c, sums[None, n_shared:], came[None, n_shared:], 0)
    place = dp * n_ctx + z

    def own_slice(v):
        return lax.dynamic_slice_in_dim(v, place * d_own, d_own, 0)

    grad_gain = own_slice(shared[:model])
    grad_shift = own_slice(shared[model : 2 * model])
    grad_bias_out = own_slice(shared[2 * model : 3 * model])
    cells = n_dp * n_seq * SEQ_LEN * model
    root_means = jnp.sqrt(shared[3 * model : 3 * model + 3] / cells)
    n_heads = head_chunks * qkv_cols
    grad_b_qkv = own[:, :n_heads].reshape(2, pairs, 3, PAIR).transpose(2, 0, 1, 3)
    grad_b_qkv = grad_b_qkv.reshape(3, heads_here, HD)
    grad_b_qkv = lax.dynamic_slice_in_dim(grad_b_qkv, place * dims_here, dims_here, 2)
    grad_b_fc1 = own[:, n_heads:].reshape(b_fc1.shape[0], HD)
    grad_b_fc1 = lax.dynamic_slice_in_dim(grad_b_fc1, place * dims_here, dims_here, 1)

    def by_owner(parts):
        whole = jnp.stack([p.reshape(2, d_own, -1) for p in parts], axis=1)
        mine = lax.dynamic_index_in_dim(whole, c, 0, keepdims=True)
        other = to_core(lax.dynamic_index_in_dim(whole, 1 - c, 0, keepdims=True))
        return in_order(c, mine, other, 0)

    def join(v):
        return v.transpose(2, 0, 1, 3).reshape(d_own, -1).astype(wide)

    grad_h = by_owner(grad_heads)
    grad_w_qkv = grad_h[..., :qkv_cols].reshape(2, head_chunks, d_own, chunk_pairs, 3, PAIR)
    grad_w_qkv = grad_w_qkv.transpose(2, 4, 0, 1, 3, 5).reshape(d_own, 3, -1).astype(wide)
    grad_w_out = join(grad_h[..., qkv_cols:]).T
    return (
        block_out,
        grad_tokens,
        grad_gain,
        grad_shift,
        grad_w_qkv,
        grad_b_qkv,
        grad_w_out,
        grad_bias_out,
        join(by_owner(grad_1)),
        grad_b_fc1,
        join(by_owner(grad_2)).T,
        grad_bias_out,
        root_means,
    )


def solution(mesh):
    n_dp, n_ctx, n_mp = (mesh.shape[name] for name in ("dp", "ctx", "mp"))
    split = jax.sharding.Mesh(
        mesh.devices.reshape(n_dp // 2, 2, n_ctx, n_mp), ("x", "core", "ctx", "mp")
    )
    rows = ("x", "core")
    owners = ("x", "core", "ctx")
    return jax.shard_map(
        on_device,
        mesh=split,
        in_specs=(
            P(rows, "ctx", None),
            P(rows, None),
            P(rows, "ctx", None),
            P(owners),
            P(owners),
            P(owners, None, "mp"),
            P(None, "mp", owners),
            P("mp", owners),
            P(owners),
            P(owners, "mp"),
            P("mp", owners),
            P("mp", owners),
            P(owners),
        ),
        out_specs=(
            P(rows, "ctx", None),
            P(rows, "ctx", None),
            P(owners),
            P(owners),
            P(owners, None, "mp"),
            P(None, "mp", owners),
            P("mp", owners),
            P(owners),
            P(owners, "mp"),
            P("mp", owners),
            P("mp", owners),
            P(owners),
            P(),
        ),
        check_vma=False,
    )
```
